128 devices in a mesh: wide: 16 (over z, x), narrow: 8 (over y, core).
Axes of the slice: x: 4, y: 4, z: 4, core: 2. Of those that a mesh axis runs over, the one named last changes fastest.
Arguments:
- tokens: bfloat16 [1024, 12288], P('narrow'), may hold values from -6 to 6
- first_blocks: bfloat16 [384, 40, 128, 128], P('wide', 'narrow'), may hold values from -0.109375 to 0.109375
- second_blocks: bfloat16 [384, 40, 128, 128], P('wide', 'narrow'), may hold values from -0.0546875 to 0.0546875
- block_rows: int32 [384, 40], P('wide', 'narrow'), may hold values from 0 to 11, as said below
- block_count: int32 [384, 8], P('wide', 'narrow'), may hold values from 1 to 5, as said below
- upstream: bfloat16 [1024, 12288], P('narrow'), may hold values from -1.5 to 1.5
Outputs:
- layer_output: bfloat16 [1024, 12288], P('wide', 'narrow')
- grad_tokens: bfloat16 [1024, 12288], P('wide', 'narrow')
- first_grad: float32 [384, 40, 128, 128], P('wide', 'narrow')
- second_grad: float32 [384, 40, 128, 128], P('wide', 'narrow')
The draws below stay inside these ranges and needn't reach their ends.
Inputs may be any that keep to these rules, and one draw needn't show every extreme that they name: `block_rows`: within each panel and each group of 5 slots the values are distinct. The first block_count slots of a panel's group are kept; in every group some panel keeps all 5.
All inputs are finite; a program needn't handle non-finite values.
Results may differ from the reference program's by a relative error of at most 0.029.
Values may be sent and summed in bfloat16 or wider, within the bound.
A program may use at most 320 MiB of HBM per device.

```python
import jax
import jax.numpy as jnp
from jax import lax

D = 12288
FF = 49152
BLOCK = 128
CAP = 5
TOKEN_TOTAL = 1024
PANELS = 384
SLOTS = 40
GROUP_BLOCKS = 12
WIDE_PANELS = 24
N_WIDE = 16
N_NARROW = 8


def draw_block_rows(key, part):
    scores = jax.random.randint(key, (PANELS, N_NARROW, GROUP_BLOCKS), 0, 1 << 20)
    scores = scores * GROUP_BLOCKS + jnp.arange(GROUP_BLOCKS, dtype=jnp.int32)
    order = jnp.argsort(scores, axis=-1, stable=True)
    return order[:, :, :CAP].reshape(PANELS, SLOTS).astype(jnp.int32)


def draw_block_count(key, part):
    first_key, second_key = jax.random.split(key)
    counts = jax.random.randint(first_key, (PANELS, N_NARROW), 1, CAP + 1)
    chosen = jax.random.randint(second_key, (1, N_NARROW), 0, PANELS)
    filled = jnp.arange(PANELS, dtype=jnp.int32)[:, None] == chosen
    return jnp.where(filled, CAP, counts).astype(jnp.int32)


def steps_of(own_key, shape, cuts, low, top_value):
    loudness, own = 1.0, jax.random.fold_in(own_key, 6)
    for axis_at, shards_of in cuts:
        steps = jnp.exp(jax.random.uniform(jax.random.fold_in(own, axis_at), (shards_of,), jnp.float32, low / len(cuts), top_value / len(cuts)))
        loudness = loudness * jnp.repeat(steps, shape[axis_at] // shards_of).reshape([-1 if axis == axis_at else 1 for axis in range(len(shape))])
    return loudness


def scatter_about(own_key, extent, deviation, bound, cuts=(), kind=jnp.bfloat16):
    values = deviation * jax.random.normal(own_key, extent, jnp.float32)
    if cuts:
        values = values * steps_of(own_key, extent, cuts, -0.22, 0.18)
    return jnp.clip(values, -bound, bound).astype(kind)


def setup_inputs(seed: int = 0) -> dict:
    seeds = jax.random.split(jax.random.key(seed), 7)
    tokens = scatter_about(seeds[0], (TOKEN_TOTAL, D), 1.0, 6.0, ((0, 8),))
    first_blocks = scatter_about(seeds[1], (PANELS, SLOTS, BLOCK, BLOCK), ((CAP + 1) // 2 * BLOCK * N_NARROW) ** -0.5, 0.109375, ((0, 16), (1, 8)))
    second_blocks = scatter_about(seeds[2], (PANELS, SLOTS, BLOCK, BLOCK), (FF * (CAP + 1) // 2 // (D // BLOCK // N_NARROW)) ** -0.5, 0.0546875, ((0, 16), (1, 8)))
    block_rows = draw_block_rows(jax.random.fold_in(seeds[6], 71), 0)
    block_count = draw_block_count(jax.random.fold_in(seeds[6], 71), 0)
    upstream = scatter_about(seeds[5], (TOKEN_TOTAL, D), 0.25, 1.5, ((0, 8),))
    return {"tokens": tokens, "first_blocks": first_blocks, "second_blocks": second_blocks, "block_rows": block_rows, "block_count": block_count, "upstream": upstream}


def reference(tokens, first_blocks, second_blocks, block_rows, block_count, upstream):
    slot_index = jnp.arange(SLOTS, dtype=jnp.int32)
    group_index = slot_index // CAP
    global_rows = (group_index[None, :] * GROUP_BLOCKS + block_rows).astype(jnp.int32)
    kept_mask = ((slot_index % CAP)[None, :] < block_count[:, group_index]).astype(jnp.float32)
    token_blocks = tokens.reshape(TOKEN_TOTAL, D // BLOCK, BLOCK)
    grad_blocks = upstream.reshape(TOKEN_TOTAL, D // BLOCK, BLOCK)

    def panel_step(running, panel_data):
        output_sum, input_sum = running
        rows_here, mask_here, first_here, second_here = panel_data
        gathered = jnp.take(token_blocks, rows_here, axis=1).astype(jnp.float32)
        grad_gathered = jnp.take(grad_blocks, rows_here, axis=1).astype(jnp.float32)
        first_kept = first_here.astype(jnp.float32) * mask_here[:, None, None]
        second_kept = second_here.astype(jnp.float32) * mask_here[:, None, None]
        partial_value = jnp.einsum('tgck,gckf->gtf', gathered.reshape(TOKEN_TOTAL, N_NARROW, CAP, BLOCK), first_kept.reshape(N_NARROW, CAP, BLOCK, BLOCK))
        preact = lax.optimization_barrier(jnp.sum(lax.optimization_barrier(partial_value.astype(jnp.bfloat16)).astype(jnp.float32), axis=0))
        hidden = jax.nn.gelu(preact).astype(jnp.bfloat16)
        hidden_wide = hidden.astype(jnp.float32)
        contrib = jnp.einsum('tf,sfk->tsk', hidden_wide, second_kept)
        output_sum = output_sum.at[:, rows_here, :].add(contrib)
        grad_partial = jnp.einsum('tgck,gcfk->gtf', grad_gathered.reshape(TOKEN_TOTAL, N_NARROW, CAP, BLOCK), second_kept.reshape(N_NARROW, CAP, BLOCK, BLOCK))
        hidden_gradient = lax.optimization_barrier(jnp.sum(lax.optimization_barrier(grad_partial.astype(jnp.bfloat16)).astype(jnp.float32), axis=0))
        pullback = jax.vjp(jax.nn.gelu, preact)[1]
        grad_pre = pullback(hidden_gradient)[0].astype(jnp.bfloat16)
        grad_wide = grad_pre.astype(jnp.float32)
        second_grad = jnp.einsum('tf,tsk->sfk', hidden_wide, grad_gathered) * mask_here[:, None, None]
        first_grad = jnp.einsum('tsk,tf->skf', gathered, grad_wide) * mask_here[:, None, None]
        backward = jnp.einsum('tf,skf->tsk', grad_wide, first_kept)
        input_sum = input_sum.at[:, rows_here, :].add(backward)
        return ((output_sum, input_sum), (first_grad, second_grad))

    def group_step(running, group_data):
        output_total, input_total = running
        empty_sum = jnp.zeros((TOKEN_TOTAL, D // BLOCK, BLOCK), jnp.float32)
        (output_part, input_part), gradients = lax.scan(panel_step, (empty_sum, empty_sum), group_data)
        output_total = output_total + lax.optimization_barrier(output_part.astype(jnp.bfloat16)).astype(jnp.float32)
        input_total = input_total + lax.optimization_barrier(input_part.astype(jnp.bfloat16)).astype(jnp.float32)
        return ((output_total, input_total), gradients)
    scan_items = (global_rows.reshape(N_WIDE, WIDE_PANELS, SLOTS), kept_mask.reshape(N_WIDE, WIDE_PANELS, SLOTS), first_blocks.reshape(N_WIDE, WIDE_PANELS, SLOTS, BLOCK, BLOCK), second_blocks.reshape(N_WIDE, WIDE_PANELS, SLOTS, BLOCK, BLOCK))
    start_sum = jnp.zeros((TOKEN_TOTAL, D // BLOCK, BLOCK), jnp.float32)
    (output_total, input_total), (first_grad, second_grad) = lax.scan(group_step, (start_sum, start_sum), scan_items)
    layer_output = output_total.reshape(TOKEN_TOTAL, D).astype(jnp.bfloat16)
    grad_tokens = input_total.reshape(TOKEN_TOTAL, D).astype(jnp.bfloat16)
    return (layer_output, grad_tokens, first_grad.reshape(PANELS, SLOTS, BLOCK, BLOCK), second_grad.reshape(PANELS, SLOTS, BLOCK, BLOCK))
```

```python
import functools
import math

import jax
import jax.numpy as jnp
from jax import lax
from jax.experimental import pallas as pl
from jax.experimental.pallas import tpu as pltpu
from jax.sharding import PartitionSpec as P

MESH = pl.DeviceIdType.MESH
BLOCK = 128
PARTS = 4
ROWS = 64 // PARTS
VMEM_LIMIT = 62 * 1024 * 1024

Y_OF = ((0, 3, 1, 2), (0, 1, 3, 2))
SWAP = (0, 2, 1, 3, 4, 6, 5, 7)
PLANE = (
    (("x", 1), ("x", 3), ("z", 1), ("z", 3)),
    (("x", 3), ("x", 1), ("z", 3), ("z", 1)),
    (("z", 1), ("z", 3), ("x", 1), ("x", 3)),
    (("z", 3), ("z", 1), ("x", 3), ("x", 1)),
)


def flip(value, mask):
    if mask == 0:
        return value
    if mask == 1:
        return value + 1 - 2 * (value % 2)
    if mask == 2:
        return (value + 2) % 4
    return 3 - value


def place():
    wide, narrow = lax.axis_index("wide"), lax.axis_index("narrow")
    return wide // 4, wide % 4, narrow // 2, narrow % 2


def plane_partner(quarter, step, z, x):
    axis, mask = PLANE[quarter][3 - step]
    return (flip(z, mask), x) if axis == "z" else (z, flip(x, mask))


def plane_owner(quarter, position, z, x):
    masks = {"x": 0, "z": 0}
    for step in range(4):
        if position >> step & 1:
            axis, mask = PLANE[quarter][3 - step]
            masks[axis] ^= mask
    return flip(z, masks["z"]), flip(x, masks["x"])


def plane_position(quarter, z_bits, x_bits):
    total = 0
    for step in range(4):
        axis, mask = PLANE[quarter][3 - step]
        high, low = z_bits if axis == "z" else x_bits
        total = total + (high if mask == 3 else (high + low) % 2) * (1 << step)
    return total


def device(z, x, y, core):
    return (z * 4 + x, y * 2 + core)


def greet(partners):
    barrier = pltpu.get_barrier_semaphore()
    for partner in partners:
        pl.semaphore_signal(barrier, inc=1, device_id=partner, device_id_type=MESH)
    pl.semaphore_wait(barrier, len(partners))


def remote(src, dst, send, recv, target):
    return pltpu.make_async_remote_copy(
        src_ref=src, dst_ref=dst, send_sem=send, recv_sem=recv, device_id=target, device_id_type=MESH
    )


def gather_kernel(
    width, tok, up, xu, held, own_sem, sib_send, sib_recv, a_send, a_recv, g_send, g_recv, out_sem
):
    z, x, y, core = place()
    part = width // 4
    source, half = z // 2, z % 2
    sibling = device(z, x, y, 1 - core)
    slots = (1, 2, 3, 5, 6, 7)

    def peer(slot):
        yy = source * flip(y, Y_OF[0][slot % 4]) + (1 - source) * flip(y, Y_OF[1][slot % 4])
        return yy, (1 - core if slot >= 4 else core)

    peers = [peer(slot) for slot in slots]
    greet(
        [device(z, x, yy, cc) for yy, cc in peers]
        + [sibling]
        + [device(flip(z, 1), x, y, core), device(flip(z, 3), x, y, core)]
        + [device(z, flip(x, 1), y, core), device(z, flip(x, 3), y, core)]
    )

    def columns(yy, cc, start, size):
        return pl.ds(pl.multiple_of((yy * 2 + cc) * width + start, 128), size)

    first = []
    for s, (yy, cc) in enumerate(peers):
        cols = columns(yy, cc, x * part, part)

        def copy(ref, s=s, yy=yy, cc=cc, cols=cols):
            return remote(
                ref.at[half, :, :, cols], held.at[:, 0, s], a_send.at[s], a_recv.at[s], device(z, x, yy, cc)
            )

        @pl.when(source == 0)
        def _(copy=copy):
            copy(tok).start()

        @pl.when(source == 1)
        def _(copy=copy):
            copy(up).start()

        first.append(copy(tok))
    own, sib = [], []
    for a, ref in enumerate((tok, up)):
        for g in range(2):
            sib.append(
                remote(
                    ref.at[g, :, :, columns(y, 1 - core, 0, width)],
                    xu.at[a, :, 4, g],
                    sib_send.at[a, g],
                    sib_recv.at[a, g],
                    sibling,
                )
            )
            own.append(
                pltpu.make_async_copy(
                    ref.at[g, :, :, columns(y, core, 0, width)], xu.at[a, :, 0, g], own_sem.at[a, g]
                )
            )
    for copy in first:
        copy.wait()
    for copy in sib + own:
        copy.start()

    def spread(t, position):
        zz, xx = plane_owner(t % 4, position, z, x)
        cols = pl.ds(pl.multiple_of(xx * part, 128), part)
        for b in range(2):
            pltpu.make_async_copy(
                held.at[t, position, pl.ds(3 * b, 3)],
                xu.at[zz // 2, t, pl.ds(1 + 4 * b, 3), zz % 2, :, cols],
                out_sem,
            ).start()

    for step in range(4):
        size = 1 << step
        copies = []
        for t in range(PARTS):
            zz, xx = plane_partner(t % 4, step, z, x)
            copies.append(
                remote(
                    held.at[t, pl.ds(0, size)],
                    held.at[t, pl.ds(size, size)],
                    g_send.at[step, t],
                    g_recv.at[step, t],
                    device(zz, xx, y, core),
                )
            )
            copies[-1].start()
        for t in range(PARTS):
            for position in range(size // 2, size):
                spread(t, position)
        for copy in copies:
            copy.wait()
    for t in range(PARTS):
        for position in range(8, 16):
            spread(t, position)
    for copy in sib + own:
        copy.wait()
    pltpu.make_async_copy(held, held, out_sem).wait()


def gather_inputs(tokens, upstream):
    rows, total = tokens.shape
    width = total // 8
    shape = (2, PARTS, rows // 2 // PARTS, total)
    dma = pltpu.SemaphoreType.DMA
    return pl.pallas_call(
        functools.partial(gather_kernel, width),
        out_shape=jax.ShapeDtypeStruct((2, PARTS, 8, 2, ROWS, width), jnp.bfloat16),
        in_specs=[pl.BlockSpec(memory_space=pl.ANY)] * 2,
        out_specs=pl.BlockSpec(memory_space=pl.ANY),
        scratch_shapes=[
            pltpu.VMEM((PARTS, 16, 6, ROWS, width // 4), jnp.bfloat16),
            dma((2, 2)),
            dma((2, 2)),
            dma((2, 2)),
            dma((6,)),
            dma((6,)),
            dma((4, PARTS)),
            dma((4, PARTS)),
            dma,
        ],
        compiler_params=pltpu.CompilerParams(
            collective_id=0, has_side_effects=True, vmem_limit_bytes=VMEM_LIMIT
        ),
    )(tokens.reshape(shape), upstream.reshape(shape))


def dense_kernel(rows, count, first, second, dense_first, dense_second):
    panel = pl.program_id(0)
    dense_first[...] = jnp.zeros_like(dense_first)
    dense_second[...] = jnp.zeros_like(dense_second)
    for slot in range(first.shape[1]):

        @pl.when(slot < count[panel, 0])
        def _(slot=slot):
            at = pl.ds(pl.multiple_of(rows[panel, slot] * BLOCK, BLOCK), BLOCK)
            dense_first[at, :] = first[0, slot]
            dense_second[:, at] = second[0, slot]


def dense_weights(first, second, rows, count, width):
    panels, cap = first.shape[:2]
    hidden = panels * BLOCK
    block = pl.BlockSpec((1, cap, BLOCK, BLOCK), lambda j, *_: (j, 0, 0, 0))
    return pl.pallas_call(
        dense_kernel,
        grid_spec=pltpu.PrefetchScalarGridSpec(
            num_scalar_prefetch=2,
            grid=(panels,),
            in_specs=[block, block],
            out_specs=[
                pl.BlockSpec((width, BLOCK), lambda j, *_: (0, j)),
                pl.BlockSpec((BLOCK, width), lambda j, *_: (j, 0)),
            ],
        ),
        out_shape=[
            jax.ShapeDtypeStruct((width, hidden), jnp.bfloat16),
            jax.ShapeDtypeStruct((hidden, width), jnp.bfloat16),
        ],
    )(rows, count, first, second)


def layer_kernel(
    width,
    hidden,
    xu_in,
    first_in,
    second_in,
    out,
    grad,
    acts,
    xu,
    first,
    second,
    part,
    got4,
    got2,
    got1,
    sum3,
    sum2,
    sum1,
    sum0,
    load_sem,
    y_send,
    y_recv,
    p_send,
    p_recv,
    acts_sem,
    free_sem,
):
    z, x, y, core = place()
    tile = 256
    third = width // 2 // tile
    loads = [
        pltpu.make_async_copy(src, dst, load_sem.at[i])
        for i, (src, dst) in enumerate(((xu_in, xu), (first_in, first), (second_in, second)))
    ]
    for copy in loads:
        copy.start()
    sibling = device(z, x, y, 1 - core)
    y_partner = [[device(z, x, flip(y, m), core) for m in (3, 1)], [device(z, x, flip(y, m), core) for m in (1, 3)]]
    greet(
        [sibling]
        + y_partner[0]
        + [device(flip(z, 1), x, y, core), device(flip(z, 3), x, y, core)]
        + [device(z, flip(x, 1), y, core), device(z, flip(x, 3), y, core)]
    )
    for copy in loads:
        copy.wait()
    chunk = 16 * ROWS

    def sums_copy(step, a, t):
        if step == 2:
            src, dst, to = part.at[a, t, pl.ds(4, 4)], got4.at[a, t], sibling
        elif step == 1:
            src, dst, to = part.at[a, t, pl.ds(2, 2)], got2.at[a, t], y_partner[a][1]
        else:
            src, dst, to = part.at[a, t, pl.ds(1, 1)], got1.at[a, t], y_partner[a][0]
        return remote(src, dst, y_send.at[step, a, t], y_recv.at[step, a, t], to)

    def back_copy(step, a, t):
        to = sibling if step == 2 else y_partner[a][step]
        size = 1 << step
        return remote(
            part.at[a, t, pl.ds(0, size)],
            part.at[a, t, pl.ds(size, size)],
            y_send.at[3 + step, a, t],
            y_recv.at[3 + step, a, t],
            to,
        )

    def sums_arrive(step, a, t):
        sums_copy(step, a, t).wait()
        to = sibling if step == 2 else y_partner[a][step]
        pl.semaphore_signal(free_sem.at[step, a, t], inc=1, device_id=to, device_id_type=MESH)

    def send_back(step, a, t):
        pl.semaphore_wait(free_sem.at[step, a, t], 1)
        back_copy(step, a, t).start()

    def plane_copy(step, a, q, t):
        rows = pl.ds(q * ROWS, ROWS)
        buffer = got4.at[a, t]
        if step == 3:
            src, dst = buffer.at[pl.ds(2, 2), rows, :], sum3.at[a, t, :, rows, :]
        elif step == 2:
            src, dst = buffer.at[pl.ds(1, 1), rows, :], sum2.at[a, t, :, rows, :]
        elif step == 1:
            src, dst = buffer.at[0, rows, pl.ds(width, width)], sum1.at[a, t, rows, :]
        else:
            src, dst = buffer.at[0, rows, pl.ds(width // 2, width // 2)], sum0.at[a, t, rows, :]
        zz, xx = plane_partner(a * 2 + q, step, z, x)
        return remote(
            src, dst, p_send.at[step, a, q, t], p_recv.at[step, a, q, t], device(zz, xx, y, core)
        )

    def up(t):
        for a in range(2):

            def body(j, _, a=a):
                cols = pl.ds(pl.multiple_of(j * tile, tile), tile)
                rows = xu[a, t].reshape(chunk, width)
                if a == 0:
                    value = jnp.dot(rows, first[:, cols], preferred_element_type=jnp.float32)
                else:
                    value = lax.dot_general(
                        rows, second[cols, :], (((1,), (1,)), ((), ())), preferred_element_type=jnp.float32
                    )
                value = value.astype(jnp.bfloat16).reshape(8, 2 * ROWS, tile)
                for i in range(8):
                    part[a, t, SWAP[i], :, cols] = value[i]
                return 0

            lax.fori_loop(0, hidden // tile, body, 0)
            sums_copy(2, a, t).start()

    def add_into(t, step):
        got = (got1, got2, got4)[step]
        size = 1 << step
        for a in range(2):
            sums_arrive(step, a, t)

            def body(j, _, a=a):
                cols = pl.ds(pl.multiple_of(j * tile, tile), tile)
                total = part[a, t, :size, :, cols].astype(jnp.float32) + got[a, t, :, :, cols].astype(jnp.float32)
                part[a, t, :size, :, cols] = total.astype(jnp.bfloat16)
                return 0

            lax.fori_loop(0, hidden // tile, body, 0)
            sums_copy(step - 1, a, t).start()

    def activate(t):
        for a in range(2):
            sums_arrive(0, a, t)

        def body(j, _):
            cols = pl.ds(pl.multiple_of(j * tile, tile), tile)

            def whole(a):
                return part[a, t, 0, :, cols].astype(jnp.float32) + got1[a, t, 0, :, cols].astype(jnp.float32)

            v, g = whole(0), whole(1)
            scale = math.sqrt(2 / math.pi)
            square = v * v
            th = jnp.tanh(scale * (v + 0.044715 * square * v))
            slope = 0.5 * (1 + th) + 0.5 * v * (1 - th * th) * (scale * (1 + 3 * 0.044715 * square))
            part[0, t, 0, :, cols] = (0.5 * v * (1 + th)).astype(jnp.bfloat16)
            part[1, t, 0, :, cols] = (g * slope).astype(jnp.bfloat16)
            return 0

        lax.fori_loop(0, hidden // tile, body, 0)
        for a in range(2):
            send_back(0, a, t)

    def forward(t, step):
        for a in range(2):
            back_copy(step - 1, a, t).wait()
            send_back(step, a, t)

    def down(t):
        for a in range(2):
            back_copy(2, a, t).wait()
            pltpu.make_async_copy(part.at[a, t], acts.at[a, t], acts_sem.at[a, t]).start()
            for q in range(2):
                spots = []
                for i in range(8):
                    yy = flip(y, Y_OF[a][i % 4])
                    cc = 1 - core if i >= 4 else core
                    z_bits = ((yy // 2 + z // 2) % 2, (yy + z) % 2)
                    for r in range(2):
                        x_bits = ((cc + x // 2) % 2, (r + x) % 2)
                        spots.append(plane_position(a * 2 + q, z_bits, x_bits))

                def body(j, _, a=a, q=q, spots=spots):
                    cols = pl.ds(pl.multiple_of((q * third + j) * tile, tile), tile)
                    rows = part[a, t].reshape(chunk, hidden)
                    if a == 0:
                        value = jnp.dot(rows, second[:, cols], preferred_element_type=jnp.float32)
                    else:
                        value = lax.dot_general(
                            rows, first[cols, :], (((1,), (1,)), ((), ())), preferred_element_type=jnp.float32
                        )
                    value = value.astype(jnp.bfloat16).reshape(16, ROWS, tile)
                    for i, spot in enumerate(spots):
                        at = pl.ds(pl.multiple_of((spot % 4) * (width // 2) + j * tile, tile), tile)
                        got4[a, t, spot // 4, pl.ds(q * ROWS, ROWS), at] = value[i]
                    return 0

                lax.fori_loop(0, third, body, 0)
                plane_copy(3, a, q, t).start()

    def plane_add(t, step):
        for a in range(2):
            for q in range(2):
                plane_copy(step, a, q, t).wait()
            cols = pl.ds(0, {3: hidden, 2: hidden, 1: width, 0: width // 2}[step])
            if step == 3:
                for i in range(2):
                    got4[a, t, i] = (
                        got4[a, t, i].astype(jnp.float32) + sum3[a, t, i].astype(jnp.float32)
                    ).astype(jnp.bfloat16)
            else:
                mine = got4[a, t, 0, :, cols].astype(jnp.float32)
                theirs = sum2[a, t, 0] if step == 2 else (sum1 if step == 1 else sum0)[a, t]
                total = (mine + theirs.astype(jnp.float32)).astype(jnp.bfloat16)
                if step:
                    got4[a, t, 0, :, cols] = total
                else:
                    for q in range(2):
                        (out, grad)[a][pl.ds(t * ROWS, ROWS), pl.ds(q * (width // 2), width // 2)] = total[
                            q * ROWS : (q + 1) * ROWS
                        ]
            if step:
                for q in range(2):
                    plane_copy(step - 1, a, q, t).start()

    stages = [
        up,
        lambda t: add_into(t, 2),
        lambda t: add_into(t, 1),
        activate,
        lambda t: forward(t, 1),
        lambda t: forward(t, 2),
        down,
        lambda t: plane_add(t, 3),
        lambda t: plane_add(t, 2),
        lambda t: plane_add(t, 1),
        lambda t: plane_add(t, 0),
    ]
    for wave in range(len(stages) + PARTS - 1):
        for t in range(PARTS):
            if 0 <= wave - t < len(stages):
                stages[wave - t](t)
    for t in range(PARTS):
        for a in range(2):
            pltpu.make_async_copy(part.at[a, t], acts.at[a, t], acts_sem.at[a, t]).wait()


def layer(xu, first, second):
    width, hidden = first.shape
    dma = pltpu.SemaphoreType.DMA

    def vmem(*shape):
        return pltpu.VMEM(shape, jnp.bfloat16)

    pair, rows = (2, PARTS), 2 * ROWS
    whole = jax.ShapeDtypeStruct((64, width), jnp.bfloat16)
    return pl.pallas_call(
        functools.partial(layer_kernel, width, hidden),
        out_shape=[whole, whole, jax.ShapeDtypeStruct((*pair, 8, rows, hidden), jnp.bfloat16)],
        in_specs=[pl.BlockSpec(memory_space=pl.ANY)] * 3,
        out_specs=[
            pl.BlockSpec(memory_space=pltpu.VMEM),
            pl.BlockSpec(memory_space=pltpu.VMEM),
            pl.BlockSpec(memory_space=pl.ANY),
        ],
        scratch_shapes=[
            vmem(*xu.shape),
            vmem(*first.shape),
            vmem(*second.shape),
            vmem(*pair, 8, rows, hidden),
            vmem(*pair, 4, rows, hidden),
            vmem(*pair, 2, rows, hidden),
            vmem(*pair, 1, rows, hidden),
            vmem(*pair, 2, rows, hidden),
            vmem(*pair, 1, rows, hidden),
            vmem(*pair, rows, width),
            vmem(*pair, rows, width // 2),
            dma((3,)),
            dma((6, *pair)),
            dma((6, *pair)),
            dma((4, 2, 2, PARTS)),
            dma((4, 2, 2, PARTS)),
            dma(pair),
            pltpu.SemaphoreType.REGULAR((3, *pair)),
        ],
        compiler_params=pltpu.CompilerParams(
            collective_id=1, has_side_effects=True, vmem_limit_bytes=VMEM_LIMIT
        ),
    )(xu, first, second)


def grads_kernel(rows, count, xu, acts, first_grad, second_grad):
    panel = pl.program_id(0)
    hidden_turned = acts[0].T
    grad_turned = acts[1].T
    for slot in range(first_grad.shape[1]):
        kept = slot < count[panel, 0]

        @pl.when(kept)
        def _(slot=slot):
            at = pl.ds(pl.multiple_of(rows[panel, slot] * BLOCK, BLOCK), BLOCK)
            second_grad[0, slot] = jnp.dot(hidden_turned, xu[1, :, at], preferred_element_type=jnp.float32)
            first_grad[0, slot] = jnp.dot(grad_turned, xu[0, :, at], preferred_element_type=jnp.float32).T

        @pl.when(jnp.logical_not(kept))
        def _(slot=slot):
            second_grad[0, slot] = jnp.zeros((BLOCK, BLOCK), jnp.float32)
            first_grad[0, slot] = jnp.zeros((BLOCK, BLOCK), jnp.float32)


def weight_grads(xu, acts, rows, count):
    panels, cap = rows.shape
    tokens, width = math.prod(xu.shape[1:-1]), xu.shape[-1]
    block = pl.BlockSpec((1, cap, BLOCK, BLOCK), lambda j, *_: (j, 0, 0, 0))
    result = jax.ShapeDtypeStruct((panels, cap, BLOCK, BLOCK), jnp.float32)
    return pl.pallas_call(
        grads_kernel,
        grid_spec=pltpu.PrefetchScalarGridSpec(
            num_scalar_prefetch=2,
            grid=(panels,),
            in_specs=[
                pl.BlockSpec((2, tokens, width), lambda j, *_: (0, 0, 0)),
                pl.BlockSpec((2, tokens, BLOCK), lambda j, *_: (0, 0, j)),
            ],
            out_specs=[block, block],
        ),
        out_shape=[result, result],
        compiler_params=pltpu.CompilerParams(vmem_limit_bytes=VMEM_LIMIT),
    )(rows, count, xu.reshape(2, tokens, width), acts.reshape(2, tokens, panels * BLOCK))


def on_device(tokens, first_blocks, second_blocks, block_rows, block_count, upstream):
    width = tokens.shape[1] // lax.axis_size("narrow")
    first, second = dense_weights(first_blocks, second_blocks, block_rows, block_count, width)
    xu = gather_inputs(tokens, upstream)
    layer_output, grad_tokens, acts = layer(xu, first, second)
    first_grad, second_grad = weight_grads(xu, acts, block_rows, block_count)
    return layer_output, grad_tokens, first_grad, second_grad


def solution(mesh):
    blocks = P("wide", "narrow", None, None)
    return jax.shard_map(
        on_device,
        mesh=mesh,
        in_specs=(P("narrow", None), blocks, blocks, P("wide", "narrow"), P("wide", "narrow"), P("narrow", None)),
        out_specs=(P("wide", "narrow"), P("wide", "narrow"), blocks, blocks),
        check_vma=False,
    )
```

```python
import functools
import math

import jax
import jax.numpy as jnp
from jax import lax
from jax.experimental import pallas as pl
from jax.experimental.pallas import tpu as pltpu
from jax.sharding import PartitionSpec as P

MESH = pl.DeviceIdType.MESH
BLOCK = 128
PARTS = 4
ROWS = 64 // PARTS
GROUP = 4
VMEM_LIMIT = 62 * 1024 * 1024

Y_OF = ((0, 3, 1, 2), (0, 1, 3, 2))
SLOTS = (1, 2, 3, 5, 6, 7)
SWAP = (0, 2, 1, 3, 4, 6, 5, 7)
PLANE = (
    (("x", 1), ("x", 3), ("z", 1), ("z", 3)),
    (("x", 3), ("x", 1), ("z", 3), ("z", 1)),
    (("z", 1), ("z", 3), ("x", 1), ("x", 3)),
    (("z", 3), ("z", 1), ("x", 3), ("x", 1)),
)


def flip(value, mask):
    if mask == 0:
        return value
    if mask == 1:
        return value + 1 - 2 * (value % 2)
    if mask == 2:
        return (value + 2) % 4
    return 3 - value


def place():
    wide, narrow = lax.axis_index("wide"), lax.axis_index("narrow")
    return wide // 4, wide % 4, narrow // 2, narrow % 2


def plane_partner(quarter, step, z, x):
    axis, mask = PLANE[quarter][3 - step]
    return (flip(z, mask), x) if axis == "z" else (z, flip(x, mask))


def plane_owner(quarter, position, z, x):
    masks = {"x": 0, "z": 0}
    for step in range(4):
        if position >> step & 1:
            axis, mask = PLANE[quarter][3 - step]
            masks[axis] ^= mask
    return flip(z, masks["z"]), flip(x, masks["x"])


def plane_position(quarter, z_bits, x_bits):
    total = 0
    for step in range(4):
        axis, mask = PLANE[quarter][3 - step]
        high, low = z_bits if axis == "z" else x_bits
        total = total + (high if mask == 3 else (high + low) % 2) * (1 << step)
    return total


def device(z, x, y, core):
    return (z * 4 + x, y * 2 + core)


def greet(partners):
    barrier = pltpu.get_barrier_semaphore()
    for partner in partners:
        pl.semaphore_signal(barrier, inc=1, device_id=partner, device_id_type=MESH)
    pl.semaphore_wait(barrier, len(partners))


def remote(src, dst, send, recv, target):
    return pltpu.make_async_remote_copy(
        src_ref=src, dst_ref=dst, send_sem=send, recv_sem=recv, device_id=target, device_id_type=MESH
    )


def layer_kernel(
    width,
    hidden,
    cap,
    block_rows,
    block_count,
    tok,
    up_rows,
    first_in,
    second_in,
    out,
    grad,
    acts,
    xu_out,
    xu,
    first,
    second,
    raw_even,
    raw_odd,
    part,
    got4,
    got2,
    got1,
    sum3,
    sum2,
    sum1,
    sum0,
    load_sem,
    own_sem,
    sib_send,
    sib_recv,
    a_send,
    a_recv,
    g_send,
    g_recv,
    xu_sem,
    y_send,
    y_recv,
    p_send,
    p_recv,
    acts_sem,
    free_sem,
):
    z, x, y, core = place()
    tile = 256
    up_tile, down_tile = 512, width // 2
    chunk = 16 * ROWS
    piece = width // 4
    source, half = z // 2, z % 2
    sibling = device(z, x, y, 1 - core)
    y_partner = [[device(z, x, flip(y, m), core) for m in (3, 1)], [device(z, x, flip(y, m), core) for m in (1, 3)]]

    raw = (raw_even, raw_odd)

    def load(group):
        return [
            pltpu.make_async_copy(
                ref.at[pl.ds(group * GROUP, GROUP)],
                raw[group % 2].at[a, :, pl.ds(0, cap)],
                load_sem.at[a, group % 2],
            )
            for a, ref in enumerate((first_in, second_in))
        ]

    for group in range(2):
        for copy in load(group):
            copy.start()

    peers = []
    for slot in SLOTS:
        yy = source * flip(y, Y_OF[0][slot % 4]) + (1 - source) * flip(y, Y_OF[1][slot % 4])
        peers.append((yy, 1 - core if slot >= 4 else core))
    greet(
        [device(z, x, yy, cc) for yy, cc in peers]
        + [sibling]
        + [device(flip(z, 1), x, y, core), device(flip(z, 3), x, y, core)]
        + [device(z, flip(x, 1), y, core), device(z, flip(x, 3), y, core)]
    )

    def columns(yy, cc, start, size):
        return pl.ds(pl.multiple_of((yy * 2 + cc) * width + start, 128), size)

    first_copies = []
    for s, (yy, cc) in enumerate(peers):
        cols = columns(yy, cc, x * piece, piece)

        def copy(ref, s=s, yy=yy, cc=cc, cols=cols):
            return remote(
                ref.at[half, :, :, cols],
                part.at[0, :, 0, pl.ds(0, ROWS), pl.ds(s * piece, piece)],
                a_send.at[s],
                a_recv.at[s],
                device(z, x, yy, cc),
            )

        @pl.when(source == 0)
        def _(copy=copy):
            copy(tok).start()

        @pl.when(source == 1)
        def _(copy=copy):
            copy(up_rows).start()

        first_copies.append(copy(tok))
    near = []
    for a, ref in enumerate((tok, up_rows)):
        for g in range(2):
            near.append(
                remote(
                    ref.at[g, :, :, columns(y, 1 - core, 0, width)],
                    xu.at[a, :, 4, g],
                    sib_send.at[a, g],
                    sib_recv.at[a, g],
                    sibling,
                )
            )
            near.append(
                pltpu.make_async_copy(
                    ref.at[g, :, :, columns(y, core, 0, width)], xu.at[a, :, 0, g], own_sem.at[a, g]
                )
            )
    for copy in near:
        copy.start()
    for ref in raw:
        ref[:, :, cap] = jnp.zeros((2, GROUP, BLOCK, BLOCK), jnp.bfloat16)

    def place_blocks(group):
        for copy in load(group):
            copy.wait()

        def body(i, _):
            panel = group * GROUP + i
            across = pl.ds(pl.multiple_of(panel * BLOCK, BLOCK), BLOCK)
            for r in range(width // BLOCK):
                slot = cap
                for s in range(cap):
                    hit = jnp.logical_and(block_rows[panel, s] == r, s < block_count[panel, 0])
                    slot = jnp.where(hit, s, slot)
                first[r * BLOCK : (r + 1) * BLOCK, across] = raw[group % 2][0, i, slot]
                second[across, r * BLOCK : (r + 1) * BLOCK] = raw[group % 2][1, i, slot]
            return 0

        lax.fori_loop(0, GROUP, body, 0)
        if group + 2 < hidden // BLOCK // GROUP:
            for copy in load(group + 2):
                copy.start()

    def gather_copies(t, step):
        copies = []
        for u in range(3):
            cols = pl.ds(u * 2 * piece, 2 * piece)
            low, high = pl.ds(0, ROWS), pl.ds(ROWS, ROWS)
            if step == 0:
                src, dst = part.at[0, t, 0, low, cols], part.at[0, t, 0, high, cols]
            else:
                size = 1 << (step - 1)
                src = part.at[0, t, pl.ds(0, size), :, cols]
                dst = part.at[0, t, pl.ds(size, size), :, cols]
            zz, xx = plane_partner((t + u) % 4, step, z, x)
            copies.append(
                remote(src, dst, g_send.at[step, t, u], g_recv.at[step, t, u], device(zz, xx, y, core))
            )
        return copies

    def gather(t, step):
        if step == 0 and t == 0:
            for copy in first_copies:
                copy.wait()
        if step > 0:
            for copy in gather_copies(t, step - 1):
                copy.wait()
        for copy in gather_copies(t, step):
            copy.start()
        if t == 0 and step < 3:
            for group in range(2 * step, 2 * step + 2):
                place_blocks(group)

    def collect(t):
        for copy in gather_copies(t, 3):
            copy.wait()
        if t == 0:
            for copy in near:
                copy.wait()
        for u in range(3):
            for position in range(16):
                zz, xx = plane_owner((t + u) % 4, position, z, x)
                cols = pl.ds(pl.multiple_of(xx * piece, 128), piece)
                for s in (2 * u, 2 * u + 1):
                    xu[zz // 2, t, SLOTS[s], zz % 2, :, cols] = part[
                        0,
                        t,
                        position // 2,
                        (position % 2) * ROWS : (position % 2 + 1) * ROWS,
                        s * piece : (s + 1) * piece,
                    ]
        for a in range(2):
            pltpu.make_async_copy(xu.at[a, t], xu_out.at[a, t], xu_sem.at[a, t]).start()


    def sums_copy(step, a, t):
        if step == 2:
            src, dst, to = part.at[a, t, pl.ds(4, 4)], got4.at[a, t], sibling
        elif step == 1:
            src, dst, to = part.at[a, t, pl.ds(2, 2)], got2.at[a, t], y_partner[a][1]
        else:
            src, dst, to = part.at[a, t, pl.ds(1, 1)], got1.at[a, t], y_partner[a][0]
        return remote(src, dst, y_send.at[step, a, t], y_recv.at[step, a, t], to)

    def back_copy(step, a, t):
        to = sibling if step == 2 else y_partner[a][step]
        size = 1 << step
        return remote(
            part.at[a, t, pl.ds(0, size)],
            part.at[a, t, pl.ds(size, size)],
            y_send.at[3 + step, a, t],
            y_recv.at[3 + step, a, t],
            to,
        )

    def sums_arrive(step, a, t):
        sums_copy(step, a, t).wait()
        to = sibling if step == 2 else y_partner[a][step]
        pl.semaphore_signal(free_sem.at[step, a, t], inc=1, device_id=to, device_id_type=MESH)

    def send_back(step, a, t):
        pl.semaphore_wait(free_sem.at[step, a, t], 1)
        back_copy(step, a, t).start()

    def plane_copy(step, a, q, t):
        rows = pl.ds(q * ROWS, ROWS)
        buffer = got4.at[a, t]
        if step == 3:
            src, dst = buffer.at[pl.ds(2, 2), rows, :], sum3.at[a, t, :, rows, :]
        elif step == 2:
            src, dst = buffer.at[pl.ds(1, 1), rows, :], sum2.at[a, t, :, rows, :]
        elif step == 1:
            src, dst = buffer.at[0, rows, pl.ds(width, width)], sum1.at[a, t, rows, :]
        else:
            src, dst = buffer.at[0, rows, pl.ds(width // 2, width // 2)], sum0.at[a, t, rows, :]
        zz, xx = plane_partner(a * 2 + q, step, z, x)
        return remote(
            src, dst, p_send.at[step, a, q, t], p_recv.at[step, a, q, t], device(zz, xx, y, core)
        )

    def up(t):
        collect(t)
        for a in range(2):

            def body(j, _, a=a):
                cols = pl.ds(pl.multiple_of(j * up_tile, up_tile), up_tile)
                rows = xu[a, t].reshape(chunk, width)
                if a == 0:
                    value = jnp.dot(rows, first[:, cols], preferred_element_type=jnp.float32)
                else:
                    value = lax.dot_general(
                        rows, second[cols, :], (((1,), (1,)), ((), ())), preferred_element_type=jnp.float32
                    )
                value = value.astype(jnp.bfloat16).reshape(8, 2 * ROWS, up_tile)
                for i in range(8):
                    part[a, t, SWAP[i], :, cols] = value[i]
                return 0

            lax.fori_loop(0, hidden // up_tile, body, 0)
            sums_copy(2, a, t).start()

    def add_into(t, step):
        got = (got1, got2, got4)[step]
        size = 1 << step
        for a in range(2):
            sums_arrive(step, a, t)

            def body(j, _, a=a):
                cols = pl.ds(pl.multiple_of(j * tile, tile), tile)
                total = part[a, t, :size, :, cols].astype(jnp.float32) + got[a, t, :, :, cols].astype(jnp.float32)
                part[a, t, :size, :, cols] = total.astype(jnp.bfloat16)
                return 0

            lax.fori_loop(0, hidden // tile, body, 0)
            sums_copy(step - 1, a, t).start()

    def activate(t):
        for a in range(2):
            sums_arrive(0, a, t)

        def body(j, _):
            cols = pl.ds(pl.multiple_of(j * tile, tile), tile)

            def whole(a):
                return part[a, t, 0, :, cols].astype(jnp.float32) + got1[a, t, 0, :, cols].astype(jnp.float32)

            v, g = whole(0), whole(1)
            scale = math.sqrt(2 / math.pi)
            square = v * v
            th = jnp.tanh(scale * (v + 0.044715 * square * v))
            slope = 0.5 * (1 + th) + 0.5 * v * (1 - th * th) * (scale * (1 + 3 * 0.044715 * square))
            part[0, t, 0, :, cols] = (0.5 * v * (1 + th)).astype(jnp.bfloat16)
            part[1, t, 0, :, cols] = (g * slope).astype(jnp.bfloat16)
            return 0

        lax.fori_loop(0, hidden // tile, body, 0)
        for a in range(2):
            send_back(0, a, t)

    def forward(t, step):
        for a in range(2):
            back_copy(step - 1, a, t).wait()
            send_back(step, a, t)

    def down(t):
        for a in range(2):
            back_copy(2, a, t).wait()
            pltpu.make_async_copy(part.at[a, t], acts.at[a, t], acts_sem.at[a, t]).start()
            for q in range(2):
                spots = []
                for i in range(8):
                    yy = flip(y, Y_OF[a][i % 4])
                    cc = 1 - core if i >= 4 else core
                    z_bits = ((yy // 2 + z // 2) % 2, (yy + z) % 2)
                    for r in range(2):
                        x_bits = ((cc + x // 2) % 2, (r + x) % 2)
                        spots.append(plane_position(a * 2 + q, z_bits, x_bits))

                def body(a=a, q=q, spots=spots):
                    cols = pl.ds(pl.multiple_of(q * down_tile, down_tile), down_tile)
                    rows = part[a, t].reshape(chunk, hidden)
                    if a == 0:
                        value = jnp.dot(rows, second[:, cols], preferred_element_type=jnp.float32)
                    else:
                        value = lax.dot_general(
                            rows, first[cols, :], (((1,), (1,)), ((), ())), preferred_element_type=jnp.float32
                        )
                    value = value.astype(jnp.bfloat16).reshape(16, ROWS, down_tile)
                    for i, spot in enumerate(spots):
                        at = pl.ds(pl.multiple_of((spot % 4) * down_tile, down_tile), down_tile)
                        got4[a, t, spot // 4, pl.ds(q * ROWS, ROWS), at] = value[i]

                body()
                plane_copy(3, a, q, t).start()

    def plane_add(t, step):
        for a in range(2):
            for q in range(2):
                plane_copy(step, a, q, t).wait()
            cols = pl.ds(0, {3: hidden, 2: hidden, 1: width, 0: width // 2}[step])
            if step == 3:
                for i in range(2):
                    got4[a, t, i] = (
                        got4[a, t, i].astype(jnp.float32) + sum3[a, t, i].astype(jnp.float32)
                    ).astype(jnp.bfloat16)
            else:
                mine = got4[a, t, 0, :, cols].astype(jnp.float32)
                theirs = sum2[a, t, 0] if step == 2 else (sum1 if step == 1 else sum0)[a, t]
                total = (mine + theirs.astype(jnp.float32)).astype(jnp.bfloat16)
                if step:
                    got4[a, t, 0, :, cols] = total
                else:
                    for q in range(2):
                        (out, grad)[a][pl.ds(t * ROWS, ROWS), pl.ds(q * (width // 2), width // 2)] = total[
                            q * ROWS : (q + 1) * ROWS
                        ]
            if step:
                for q in range(2):
                    plane_copy(step - 1, a, q, t).start()

    stages = [
        lambda t: gather(t, 0),
        lambda t: gather(t, 1),
        lambda t: gather(t, 2),
        lambda t: gather(t, 3),
        up,
        lambda t: add_into(t, 2),
        lambda t: add_into(t, 1),
        activate,
        lambda t: forward(t, 1),
        lambda t: forward(t, 2),
        down,
        lambda t: plane_add(t, 3),
        lambda t: plane_add(t, 2),
        lambda t: plane_add(t, 1),
        lambda t: plane_add(t, 0),
    ]
    turn = [0, 0, 0, 0, 1, 0, 2, 2, 2, 2, 1, 2, 2, 2, 2]
    for wave in range(len(stages) + PARTS - 1):
        now = [t for t in range(PARTS) if 0 <= wave - t < len(stages)]
        for t in sorted(now, key=lambda t: (turn[wave - t], -t if wave - t > 4 else t)):
            stages[wave - t](t)
    for t in range(PARTS):
        for a in range(2):
            pltpu.make_async_copy(part.at[a, t], acts.at[a, t], acts_sem.at[a, t]).wait()
            pltpu.make_async_copy(xu.at[a, t], xu_out.at[a, t], xu_sem.at[a, t]).wait()


def layer(tokens, upstream, first_blocks, second_blocks, rows_of, count):
    local, total = tokens.shape
    panels, cap = first_blocks.shape[:2]
    width, hidden = total // 8, panels * BLOCK
    split = (2, PARTS, local // 2 // PARTS, total)
    dma = pltpu.SemaphoreType.DMA

    def vmem(*shape):
        return pltpu.VMEM(shape, jnp.bfloat16)

    pair, rows = (2, PARTS), 2 * ROWS
    inputs = (*pair, 8, 2, ROWS, width)
    whole = jax.ShapeDtypeStruct((64, width), jnp.bfloat16)
    anywhere = pl.BlockSpec(memory_space=pl.ANY)
    scalars = pl.BlockSpec(memory_space=pltpu.SMEM)
    on_chip = pl.BlockSpec(memory_space=pltpu.VMEM)
    return pl.pallas_call(
        functools.partial(layer_kernel, width, hidden, cap),
        out_shape=[
            whole,
            whole,
            jax.ShapeDtypeStruct((*pair, 8, rows, hidden), jnp.bfloat16),
            jax.ShapeDtypeStruct(inputs, jnp.bfloat16),
        ],
        in_specs=[scalars, scalars] + [anywhere] * 4,
        out_specs=[on_chip, on_chip, anywhere, anywhere],
        scratch_shapes=[
            vmem(*inputs),
            vmem(width, hidden),
            vmem(hidden, width),
            vmem(2, GROUP, cap + 1, BLOCK, BLOCK),
            vmem(2, GROUP, cap + 1, BLOCK, BLOCK),
            vmem(*pair, 8, rows, hidden),
            vmem(*pair, 4, rows, hidden),
            vmem(*pair, 2, rows, hidden),
            vmem(*pair, 1, rows, hidden),
            vmem(*pair, 2, rows, hidden),
            vmem(*pair, 1, rows, hidden),
            vmem(*pair, rows, width),
            vmem(*pair, rows, width // 2),
            dma((2, 2)),
            dma((2, 2)),
            dma((2, 2)),
            dma((2, 2)),
            dma((6,)),
            dma((6,)),
            dma((4, PARTS, 3)),
            dma((4, PARTS, 3)),
            dma(pair),
            dma((6, *pair)),
            dma((6, *pair)),
            dma((4, 2, 2, PARTS)),
            dma((4, 2, 2, PARTS)),
            dma(pair),
            pltpu.SemaphoreType.REGULAR((3, *pair)),
        ],
        compiler_params=pltpu.CompilerParams(
            collective_id=1, has_side_effects=True, vmem_limit_bytes=VMEM_LIMIT
        ),
    )(rows_of, count, tokens.reshape(split), upstream.reshape(split), first_blocks, second_blocks)


def grads_kernel(rows, count, xu, acts, first_grad, second_grad, turned):
    panel = pl.program_id(0)
    cap = first_grad.shape[1]

    @pl.when(panel == 0)
    def _():
        def body(r, _):
            at = pl.ds(pl.multiple_of(r * BLOCK, BLOCK), BLOCK)
            for a in range(2):
                turned[a, at, :] = xu[a, :, at].T
            return 0

        lax.fori_loop(0, xu.shape[2] // BLOCK, body, 0)

    def one(p, _):
        at_panel = pl.ds(pl.multiple_of(p * BLOCK, BLOCK), BLOCK)
        index = panel * first_grad.shape[0] + p
        for kept in range(1, cap + 1):

            @pl.when(count[index, 0] == kept)
            def _(kept=kept):
                for a, grad in ((0, first_grad), (1, second_grad)):
                    blocks = [
                        turned[a, pl.ds(pl.multiple_of(rows[index, slot] * BLOCK, BLOCK), BLOCK), :]
                        for slot in range(kept)
                    ]
                    value = jnp.dot(
                        jnp.concatenate(blocks), acts[1 - a, :, at_panel], preferred_element_type=jnp.float32
                    )
                    for slot in range(cap):
                        if slot >= kept:
                            grad[p, slot] = jnp.zeros((BLOCK, BLOCK), jnp.float32)
                        else:
                            block = value[slot * BLOCK : (slot + 1) * BLOCK]
                            grad[p, slot] = block.T if a else block

        return 0

    lax.fori_loop(0, first_grad.shape[0], one, 0)


def weight_grads(xu, acts, rows, count):
    panels, cap = rows.shape
    tokens, width = math.prod(xu.shape[1:-1]), xu.shape[-1]
    block = pl.BlockSpec((GROUP, cap, BLOCK, BLOCK), lambda j, *_: (j, 0, 0, 0))
    result = jax.ShapeDtypeStruct((panels, cap, BLOCK, BLOCK), jnp.float32)
    return pl.pallas_call(
        grads_kernel,
        grid_spec=pltpu.PrefetchScalarGridSpec(
            num_scalar_prefetch=2,
            grid=(panels // GROUP,),
            in_specs=[
                pl.BlockSpec((2, tokens, width), lambda j, *_: (0, 0, 0)),
                pl.BlockSpec((2, tokens, GROUP * BLOCK), lambda j, *_: (0, 0, j)),
            ],
            out_specs=[block, block],
            scratch_shapes=[pltpu.VMEM((2, width, tokens), jnp.bfloat16)],
        ),
        out_shape=[result, result],
        compiler_params=pltpu.CompilerParams(vmem_limit_bytes=VMEM_LIMIT),
    )(rows, count, xu.reshape(2, tokens, width), acts.reshape(2, tokens, panels * BLOCK))


def on_device(tokens, first_blocks, second_blocks, block_rows, block_count, upstream):
    layer_output, grad_tokens, acts, xu = layer(
        tokens, upstream, first_blocks, second_blocks, block_rows, block_count
    )
    first_grad, second_grad = weight_grads(xu, acts, block_rows, block_count)
    return layer_output, grad_tokens, first_grad, second_grad


def solution(mesh):
    blocks = P("wide", "narrow", None, None)
    return jax.shard_map(
        on_device,
        mesh=mesh,
        in_specs=(P("narrow", None), blocks, blocks, P("wide", "narrow"), P("wide", "narrow"), P("narrow", None)),
        out_specs=(P("wide", "narrow"), P("wide", "narrow"), blocks, blocks),
        check_vma=False,
    )
```

```python
import functools
import math

import jax
import jax.numpy as jnp
from jax import lax
from jax.experimental import pallas as pl
from jax.experimental.pallas import tpu as pltpu
from jax.sharding import PartitionSpec as P

MESH = pl.DeviceIdType.MESH
BLOCK = 128
PARTS = 4
ROWS = 64 // PARTS
GROUP = 4
VMEM_LIMIT = 62 * 1024 * 1024

Y_OF = ((0, 3, 1, 2), (0, 1, 3, 2))
SLOTS = (1, 2, 3, 5, 6, 7)
SWAP = (0, 2, 1, 3, 4, 6, 5, 7)
PLANE = (
    (("x", 1), ("x", 3), ("z", 1), ("z", 3)),
    (("x", 3), ("x", 1), ("z", 3), ("z", 1)),
    (("z", 1), ("z", 3), ("x", 1), ("x", 3)),
    (("z", 3), ("z", 1), ("x", 3), ("x", 1)),
)

ORDER = (
    ("dens", 0, 0), ("dens", 1, 0), ("g0", 0, 0), ("g0", 1, 0), ("g1", 0, 0), ("g1", 1, 0),
    ("g0", 2, 0), ("g2", 0, 0), ("dens", 2, 0), ("g3", 0, 0), ("dens", 3, 0), ("dens", 4, 0),
    ("dens", 5, 0), ("g1", 2, 0), ("g2", 1, 0), ("col", 0, 0), ("up", 0, 1), ("g3", 1, 0),
    ("up", 0, 0), ("s1", 0, 1), ("g0", 3, 0), ("s1", 0, 0), ("g2", 2, 0), ("col", 1, 0),
    ("up", 1, 1), ("up", 1, 0), ("s1", 1, 1), ("s2", 0, 1), ("g3", 2, 0), ("s2", 0, 0),
    ("s1", 1, 0), ("col", 2, 0), ("g1", 3, 0), ("up", 2, 1), ("act", 0, 0), ("s2", 1, 1),
    ("g2", 3, 0), ("s1", 2, 1), ("up", 2, 0), ("f1", 0, 1), ("s1", 2, 0), ("g3", 3, 0),
    ("s2", 2, 1), ("f1", 0, 0), ("col", 3, 0), ("s2", 2, 0), ("up", 3, 1), ("f2", 0, 1),
    ("s2", 1, 0), ("up", 3, 0), ("s1", 3, 1), ("act", 2, 0), ("s1", 3, 0), ("f2", 0, 0),
    ("f1", 2, 1), ("f1", 2, 0), ("d", 0, 0), ("d", 0, 1), ("act", 1, 0), ("p3", 0, 1),
    ("s2", 3, 0), ("s2", 3, 1), ("f2", 2, 1), ("p2", 0, 1), ("p3", 0, 0), ("f1", 1, 1),
    ("f2", 2, 0), ("f1", 1, 0), ("d", 2, 1), ("d", 2, 0), ("p1", 0, 1), ("p2", 0, 0),
    ("act", 3, 0), ("f2", 1, 1), ("p3", 2, 1), ("f2", 1, 0), ("p3", 2, 0), ("f1", 3, 0),
    ("d", 1, 1), ("f1", 3, 1), ("d", 1, 0), ("f2", 3, 0), ("p1", 0, 0), ("p2", 2, 0),
    ("p3", 1, 1), ("p3", 1, 0), ("f2", 3, 1), ("d", 3, 0), ("p2", 1, 0), ("d", 3, 1),
    ("p2", 2, 1), ("p2", 1, 1), ("p1", 2, 1), ("p1", 2, 0), ("p1", 1, 0), ("p3", 3, 0),
    ("p3", 3, 1), ("p0", 1, 0), ("p0", 0, 0), ("p0", 2, 1), ("p1", 1, 1), ("p2", 3, 0),
    ("p2", 3, 1), ("p1", 3, 0), ("p1", 3, 1), ("p0", 0, 1), ("p0", 2, 0), ("p0", 1, 1),
    ("p0", 3, 0), ("p0", 3, 1),
)


def flip(value, mask):
    if mask == 0:
        return value
    if mask == 1:
        return value + 1 - 2 * (value % 2)
    if mask == 2:
        return (value + 2) % 4
    return 3 - value


def place():
    wide, narrow = lax.axis_index("wide"), lax.axis_index("narrow")
    return wide // 4, wide % 4, narrow // 2, narrow % 2


def plane_partner(quarter, step, z, x):
    axis, mask = PLANE[quarter][3 - step]
    return (flip(z, mask), x) if axis == "z" else (z, flip(x, mask))


def plane_owner(quarter, position, z, x):
    masks = {"x": 0, "z": 0}
    for step in range(4):
        if position >> step & 1:
            axis, mask = PLANE[quarter][3 - step]
            masks[axis] ^= mask
    return flip(z, masks["z"]), flip(x, masks["x"])


def plane_position(quarter, z_bits, x_bits):
    total = 0
    for step in range(4):
        axis, mask = PLANE[quarter][3 - step]
        high, low = z_bits if axis == "z" else x_bits
        total = total + (high if mask == 3 else (high + low) % 2) * (1 << step)
    return total


def device(z, x, y, core):
    return (z * 4 + x, y * 2 + core)


def greet(partners):
    barrier = pltpu.get_barrier_semaphore()
    for partner in partners:
        pl.semaphore_signal(barrier, inc=1, device_id=partner, device_id_type=MESH)
    pl.semaphore_wait(barrier, len(partners))


def remote(src, dst, send, recv, target):
    return pltpu.make_async_remote_copy(
        src_ref=src, dst_ref=dst, send_sem=send, recv_sem=recv, device_id=target, device_id_type=MESH
    )


def layer_kernel(
    width,
    hidden,
    cap,
    block_rows,
    block_count,
    tok,
    up_rows,
    first_in,
    second_in,
    out,
    grad,
    acts,
    xt,
    xu,
    first,
    second,
    raw_even,
    raw_odd,
    part,
    turned,
    got4,
    got2,
    got1,
    sum3,
    sum2,
    sum1,
    sum0,
    load_sem,
    own_sem,
    sib_send,
    sib_recv,
    a_send,
    a_recv,
    g_send,
    g_recv,
    xt_sem,
    y_send,
    y_recv,
    p_send,
    p_recv,
    acts_sem,
    free_sem,
):
    z, x, y, core = place()
    tile = 256
    up_tile, down_tile = 512, width // 2
    chunk = 16 * ROWS
    piece = width // 4
    source, half = z // 2, z % 2
    sibling = device(z, x, y, 1 - core)
    y_partner = [[device(z, x, flip(y, m), core) for m in (3, 1)], [device(z, x, flip(y, m), core) for m in (1, 3)]]

    raw = (raw_even, raw_odd)

    def load(group):
        return [
            pltpu.make_async_copy(
                ref.at[pl.ds(group * GROUP, GROUP)],
                raw[group % 2].at[a, :, pl.ds(0, cap)],
                load_sem.at[a, group % 2],
            )
            for a, ref in enumerate((first_in, second_in))
        ]

    for group in range(2):
        for copy in load(group):
            copy.start()

    peers = []
    for slot in SLOTS:
        yy = source * flip(y, Y_OF[0][slot % 4]) + (1 - source) * flip(y, Y_OF[1][slot % 4])
        peers.append((yy, 1 - core if slot >= 4 else core))
    greet(
        [device(z, x, yy, cc) for yy, cc in peers]
        + [sibling]
        + [device(flip(z, 1), x, y, core), device(flip(z, 3), x, y, core)]
        + [device(z, flip(x, 1), y, core), device(z, flip(x, 3), y, core)]
    )

    def columns(yy, cc, start, size):
        return pl.ds(pl.multiple_of((yy * 2 + cc) * width + start, 128), size)

    first_copies = [[] for _ in range(PARTS)]
    for t in range(PARTS):
        for s, (yy, cc) in enumerate(peers):
            cols = columns(yy, cc, x * piece, piece)

            def copy(ref, t=t, s=s, yy=yy, cc=cc, cols=cols):
                return remote(
                    ref.at[half, t, :, cols],
                    part.at[0, t, 0, pl.ds(0, ROWS), pl.ds(s * piece, piece)],
                    a_send.at[s, t],
                    a_recv.at[s, t],
                    device(z, x, yy, cc),
                )

            @pl.when(source == 0)
            def _(copy=copy):
                copy(tok).start()

            @pl.when(source == 1)
            def _(copy=copy):
                copy(up_rows).start()

            first_copies[t].append(copy(tok))
    near = []
    for a, ref in enumerate((tok, up_rows)):
        for g in range(2):
            near.append(
                remote(
                    ref.at[g, :, :, columns(y, 1 - core, 0, width)],
                    xu.at[a, :, 4, g],
                    sib_send.at[a, g],
                    sib_recv.at[a, g],
                    sibling,
                )
            )
            near.append(
                pltpu.make_async_copy(
                    ref.at[g, :, :, columns(y, core, 0, width)], xu.at[a, :, 0, g], own_sem.at[a, g]
                )
            )
    for copy in near:
        copy.start()
    for ref in raw:
        ref[:, :, cap] = jnp.zeros((2, GROUP, BLOCK, BLOCK), jnp.bfloat16)

    def place_blocks(group):
        for copy in load(group):
            copy.wait()

        def body(i, _):
            panel = group * GROUP + i
            across = pl.ds(pl.multiple_of(panel * BLOCK, BLOCK), BLOCK)
            for r in range(width // BLOCK):
                slot = cap
                for s in range(cap):
                    hit = jnp.logical_and(block_rows[s, panel] == r, s < block_count[panel])
                    slot = jnp.where(hit, s, slot)
                first[r * BLOCK : (r + 1) * BLOCK, across] = raw[group % 2][0, i, slot]
                second[across, r * BLOCK : (r + 1) * BLOCK] = raw[group % 2][1, i, slot]
            return 0

        lax.fori_loop(0, GROUP, body, 0)
        if group + 2 < hidden // BLOCK // GROUP:
            for copy in load(group + 2):
                copy.start()

    def gather_copies(t, step):
        copies = []
        for u in range(3):
            cols = pl.ds(u * 2 * piece, 2 * piece)
            low, high = pl.ds(0, ROWS), pl.ds(ROWS, ROWS)
            if step == 0:
                src, dst = part.at[0, t, 0, low, cols], part.at[0, t, 0, high, cols]
            else:
                size = 1 << (step - 1)
                src = part.at[0, t, pl.ds(0, size), :, cols]
                dst = part.at[0, t, pl.ds(size, size), :, cols]
            zz, xx = plane_partner((t + u) % 4, step, z, x)
            copies.append(
                remote(src, dst, g_send.at[step, t, u], g_recv.at[step, t, u], device(zz, xx, y, core))
            )
        return copies

    def gather(t, step):
        if step == 0:
            for copy in first_copies[t]:
                copy.wait()
        if step > 0:
            for copy in gather_copies(t, step - 1):
                copy.wait()
        for copy in gather_copies(t, step):
            copy.start()

    def collect(t):
        for copy in gather_copies(t, 3):
            copy.wait()
        while near:
            near.pop().wait()
        for u in range(3):
            for position in range(16):
                zz, xx = plane_owner((t + u) % 4, position, z, x)
                cols = pl.ds(pl.multiple_of(xx * piece, 128), piece)
                for s in (2 * u, 2 * u + 1):
                    xu[zz // 2, t, SLOTS[s], zz % 2, :, cols] = part[
                        0,
                        t,
                        position // 2,
                        (position % 2) * ROWS : (position % 2 + 1) * ROWS,
                        s * piece : (s + 1) * piece,
                    ]

    turning = []

    def turn_copies(t):
        cols = pl.ds(t * chunk, chunk)
        return [pltpu.make_async_copy(turned.at[a], xt.at[a, :, cols], xt_sem.at[a]) for a in range(2)]

    def turn_inputs(t):
        while turning:
            turning.pop().wait()
        for a in range(2):
            turned[a] = xu[a, t].reshape(chunk, width).T
        for copy in turn_copies(t):
            copy.start()
            turning.append(copy)

    def sums_copy(step, a, t):
        if step == 2:
            src, dst, to = part.at[a, t, pl.ds(4, 4)], got4.at[a, t], sibling
        elif step == 1:
            src, dst, to = part.at[a, t, pl.ds(2, 2)], got2.at[a, t], y_partner[a][1]
        else:
            src, dst, to = part.at[a, t, pl.ds(1, 1)], got1.at[a, t], y_partner[a][0]
        return remote(src, dst, y_send.at[step, a, t], y_recv.at[step, a, t], to)

    def back_copy(step, a, t):
        to = sibling if step == 2 else y_partner[a][step]
        size = 1 << step
        return remote(
            part.at[a, t, pl.ds(0, size)],
            part.at[a, t, pl.ds(size, size)],
            y_send.at[3 + step, a, t],
            y_recv.at[3 + step, a, t],
            to,
        )

    def sums_arrive(step, a, t):
        sums_copy(step, a, t).wait()
        to = sibling if step == 2 else y_partner[a][step]
        pl.semaphore_signal(free_sem.at[step, a, t], inc=1, device_id=to, device_id_type=MESH)

    def send_back(step, a, t):
        pl.semaphore_wait(free_sem.at[step, a, t], 1)
        back_copy(step, a, t).start()

    def plane_copy(step, a, q, t):
        rows = pl.ds(q * ROWS, ROWS)
        buffer = got4.at[a, t]
        if step == 3:
            src, dst = buffer.at[pl.ds(2, 2), rows, :], sum3.at[a, t, :, rows, :]
        elif step == 2:
            src, dst = buffer.at[pl.ds(1, 1), rows, :], sum2.at[a, t, :, rows, :]
        elif step == 1:
            src, dst = buffer.at[0, rows, pl.ds(width, width)], sum1.at[a, t, rows, :]
        else:
            src, dst = buffer.at[0, rows, pl.ds(width // 2, width // 2)], sum0.at[a, t, rows, :]
        zz, xx = plane_partner(a * 2 + q, step, z, x)
        return remote(
            src, dst, p_send.at[step, a, q, t], p_recv.at[step, a, q, t], device(zz, xx, y, core)
        )

    def up(t, a):

        def body(j, _, a=a):
            cols = pl.ds(pl.multiple_of(j * up_tile, up_tile), up_tile)
            rows = xu[a, t].reshape(chunk, width)
            if a == 0:
                value = jnp.dot(rows, first[:, cols], preferred_element_type=jnp.float32)
            else:
                value = lax.dot_general(
                    rows, second[cols, :], (((1,), (1,)), ((), ())), preferred_element_type=jnp.float32
                )
            value = value.astype(jnp.bfloat16).reshape(8, 2 * ROWS, up_tile)
            for i in range(8):
                part[a, t, SWAP[i], :, cols] = value[i]
            return 0

        lax.fori_loop(0, hidden // up_tile, body, 0)
        sums_copy(2, a, t).start()

    def add_into(t, a, step):
        got = (got1, got2, got4)[step]
        size = 1 << step
        sums_arrive(step, a, t)

        def body(j, _, a=a):
            cols = pl.ds(pl.multiple_of(j * tile, tile), tile)
            total = part[a, t, :size, :, cols].astype(jnp.float32) + got[a, t, :, :, cols].astype(jnp.float32)
            part[a, t, :size, :, cols] = total.astype(jnp.bfloat16)
            return 0

        lax.fori_loop(0, hidden // tile, body, 0)
        sums_copy(step - 1, a, t).start()

    def activate(t):
        for a in range(2):
            sums_arrive(0, a, t)

        def body(j, _):
            cols = pl.ds(pl.multiple_of(j * tile, tile), tile)

            def whole(a):
                return part[a, t, 0, :, cols].astype(jnp.float32) + got1[a, t, 0, :, cols].astype(jnp.float32)

            v, g = whole(0), whole(1)
            scale = math.sqrt(2 / math.pi)
            square = v * v
            th = jnp.tanh(scale * (v + 0.044715 * square * v))
            slope = 0.5 * (1 + th) + 0.5 * v * (1 - th * th) * (scale * (1 + 3 * 0.044715 * square))
            part[0, t, 0, :, cols] = (0.5 * v * (1 + th)).astype(jnp.bfloat16)
            part[1, t, 0, :, cols] = (g * slope).astype(jnp.bfloat16)
            return 0

        lax.fori_loop(0, hidden // tile, body, 0)
        for a in range(2):
            send_back(0, a, t)
        turn_inputs(t)

    def forward(t, a, step):
        back_copy(step - 1, a, t).wait()
        send_back(step, a, t)

    def down(t, a):
        back_copy(2, a, t).wait()
        pltpu.make_async_copy(part.at[a, t], acts.at[a, t], acts_sem.at[a, t]).start()
        for q in range(2):
            spots = []
            for i in range(8):
                yy = flip(y, Y_OF[a][i % 4])
                cc = 1 - core if i >= 4 else core
                z_bits = ((yy // 2 + z // 2) % 2, (yy + z) % 2)
                for r in range(2):
                    x_bits = ((cc + x // 2) % 2, (r + x) % 2)
                    spots.append(plane_position(a * 2 + q, z_bits, x_bits))

            def body(a=a, q=q, spots=spots):
                cols = pl.ds(pl.multiple_of(q * down_tile, down_tile), down_tile)
                rows = part[a, t].reshape(chunk, hidden)
                if a == 0:
                    value = jnp.dot(rows, second[:, cols], preferred_element_type=jnp.float32)
                else:
                    value = lax.dot_general(
                        rows, first[cols, :], (((1,), (1,)), ((), ())), preferred_element_type=jnp.float32
                    )
                value = value.astype(jnp.bfloat16).reshape(16, ROWS, down_tile)
                for i, spot in enumerate(spots):
                    at = pl.ds(pl.multiple_of((spot % 4) * down_tile, down_tile), down_tile)
                    got4[a, t, spot // 4, pl.ds(q * ROWS, ROWS), at] = value[i]

            body()
            plane_copy(3, a, q, t).start()

    def plane_add(t, a, step):
        for q in range(2):
            plane_copy(step, a, q, t).wait()
        cols = pl.ds(0, {3: hidden, 2: hidden, 1: width, 0: width // 2}[step])
        if step == 3:
            for i in range(2):
                got4[a, t, i] = (
                    got4[a, t, i].astype(jnp.float32) + sum3[a, t, i].astype(jnp.float32)
                ).astype(jnp.bfloat16)
        else:
            mine = got4[a, t, 0, :, cols].astype(jnp.float32)
            theirs = sum2[a, t, 0] if step == 2 else (sum1 if step == 1 else sum0)[a, t]
            total = (mine + theirs.astype(jnp.float32)).astype(jnp.bfloat16)
            if step:
                got4[a, t, 0, :, cols] = total
            else:
                for q in range(2):
                    (out, grad)[a][pl.ds(t * ROWS, ROWS), pl.ds(q * (width // 2), width // 2)] = total[
                        q * ROWS : (q + 1) * ROWS
                    ]
        if step:
            for q in range(2):
                plane_copy(step - 1, a, q, t).start()

    stages = {
        "up": up,
        "s1": lambda t, a: add_into(t, a, 2),
        "s2": lambda t, a: add_into(t, a, 1),
        "act": lambda t, a: activate(t),
        "f1": lambda t, a: forward(t, a, 1),
        "f2": lambda t, a: forward(t, a, 2),
        "d": down,
        "dens": lambda group, a: place_blocks(group),
        "col": lambda t, a: collect(t),
    }
    for step in range(4):
        stages[f"g{step}"] = lambda t, a, step=step: gather(t, step)
        stages[f"p{step}"] = lambda t, a, step=step: plane_add(t, a, step)
    for name, t, a in ORDER:
        stages[name](t, a)
    for t in range(PARTS):
        for a in range(2):
            pltpu.make_async_copy(part.at[a, t], acts.at[a, t], acts_sem.at[a, t]).wait()
    while turning:
        turning.pop().wait()


def layer(tokens, upstream, first_blocks, second_blocks, rows_of, count):
    local, total = tokens.shape
    panels, cap = first_blocks.shape[:2]
    width, hidden = total // 8, panels * BLOCK
    split = (2, PARTS, local // 2 // PARTS, total)
    dma = pltpu.SemaphoreType.DMA

    def vmem(*shape):
        return pltpu.VMEM(shape, jnp.bfloat16)

    pair, rows = (2, PARTS), 2 * ROWS
    inputs = (*pair, 8, 2, ROWS, width)
    whole = jax.ShapeDtypeStruct((64, width), jnp.bfloat16)
    anywhere = pl.BlockSpec(memory_space=pl.ANY)
    scalars = pl.BlockSpec(memory_space=pltpu.SMEM)
    on_chip = pl.BlockSpec(memory_space=pltpu.VMEM)
    return pl.pallas_call(
        functools.partial(layer_kernel, width, hidden, cap),
        out_shape=[
            whole,
            whole,
            jax.ShapeDtypeStruct((*pair, 8, rows, hidden), jnp.bfloat16),
            jax.ShapeDtypeStruct((2, width, 16 * ROWS * PARTS), jnp.bfloat16),
        ],
        in_specs=[scalars, scalars] + [anywhere] * 4,
        out_specs=[on_chip, on_chip, anywhere, anywhere],
        scratch_shapes=[
            vmem(*inputs),
            vmem(width, hidden),
            vmem(hidden, width),
            vmem(2, GROUP, cap + 1, BLOCK, BLOCK),
            vmem(2, GROUP, cap + 1, BLOCK, BLOCK),
            vmem(*pair, 8, rows, hidden),
            vmem(2, width, 16 * ROWS),
            vmem(*pair, 4, rows, hidden),
            vmem(*pair, 2, rows, hidden),
            vmem(*pair, 1, rows, hidden),
            vmem(*pair, 2, rows, hidden),
            vmem(*pair, 1, rows, hidden),
            vmem(*pair, rows, width),
            vmem(*pair, rows, width // 2),
            dma((2, 2)),
            dma((2, 2)),
            dma((2, 2)),
            dma((2, 2)),
            dma((6, PARTS)),
            dma((6, PARTS)),
            dma((4, PARTS, 3)),
            dma((4, PARTS, 3)),
            dma((2,)),
            dma((6, *pair)),
            dma((6, *pair)),
            dma((4, 2, 2, PARTS)),
            dma((4, 2, 2, PARTS)),
            dma(pair),
            pltpu.SemaphoreType.REGULAR((3, *pair)),
        ],
        compiler_params=pltpu.CompilerParams(
            collective_id=1, has_side_effects=True, vmem_limit_bytes=VMEM_LIMIT
        ),
    )(rows_of, count, tokens.reshape(split), upstream.reshape(split), first_blocks, second_blocks)


def grads_kernel(rows, count, xt, acts, first_grad, second_grad):
    panel = pl.program_id(0)
    cap = first_grad.shape[1]

    def one(p, _):
        at_panel = pl.ds(pl.multiple_of(p * BLOCK, BLOCK), BLOCK)
        index = panel * first_grad.shape[0] + p
        for kept in range(1, cap + 1):

            @pl.when(count[index] == kept)
            def _(kept=kept):
                for a, grad in ((0, first_grad), (1, second_grad)):
                    blocks = [
                        xt[a, pl.ds(pl.multiple_of(rows[slot, index] * BLOCK, BLOCK), BLOCK), :]
                        for slot in range(kept)
                    ]
                    value = jnp.dot(
                        jnp.concatenate(blocks), acts[1 - a, :, at_panel], preferred_element_type=jnp.float32
                    )
                    for slot in range(cap):
                        if slot >= kept:
                            grad[p, slot] = jnp.zeros((BLOCK, BLOCK), jnp.float32)
                        else:
                            block = value[slot * BLOCK : (slot + 1) * BLOCK]
                            grad[p, slot] = block.T if a else block

        return 0

    lax.fori_loop(0, first_grad.shape[0], one, 0)


def weight_grads(xt, acts, rows, count):
    cap, panels = rows.shape
    _, width, tokens = xt.shape
    block = pl.BlockSpec((GROUP, cap, BLOCK, BLOCK), lambda j, *_: (j, 0, 0, 0))
    result = jax.ShapeDtypeStruct((panels, cap, BLOCK, BLOCK), jnp.float32)
    return pl.pallas_call(
        grads_kernel,
        grid_spec=pltpu.PrefetchScalarGridSpec(
            num_scalar_prefetch=2,
            grid=(panels // GROUP,),
            in_specs=[
                pl.BlockSpec((2, width, tokens), lambda j, *_: (0, 0, 0)),
                pl.BlockSpec((2, tokens, GROUP * BLOCK), lambda j, *_: (0, 0, j)),
            ],
            out_specs=[block, block],
        ),
        out_shape=[result, result],
        compiler_params=pltpu.CompilerParams(vmem_limit_bytes=VMEM_LIMIT),
    )(rows, count, xt, acts.reshape(2, tokens, panels * BLOCK))


def on_device(tokens, first_blocks, second_blocks, block_rows, block_count, upstream):
    rows, count = block_rows.T, block_count.reshape(-1)
    layer_output, grad_tokens, acts, xt = layer(tokens, upstream, first_blocks, second_blocks, rows, count)
    first_grad, second_grad = weight_grads(xt, acts, rows, count)
    return layer_output, grad_tokens, first_grad, second_grad


def solution(mesh):
    blocks = P("wide", "narrow", None, None)
    return jax.shard_map(
        on_device,
        mesh=mesh,
        in_specs=(P("narrow", None), blocks, blocks, P("wide", "narrow"), P("wide", "narrow"), P("narrow", None)),
        out_specs=(P("wide", "narrow"), P("wide", "narrow"), blocks, blocks),
        check_vma=False,
    )
```

```python
import functools
import math

import jax
import jax.numpy as jnp
from jax import lax
from jax.experimental import pallas as pl
from jax.experimental.pallas import tpu as pltpu
from jax.sharding import PartitionSpec as P

MESH = pl.DeviceIdType.MESH
BLOCK = 128
PARTS = 4
ROWS = 64 // PARTS
GROUP = 4
VMEM_LIMIT = 62 * 1024 * 1024

Y_OF = ((0, 3, 1, 2), (0, 1, 3, 2))
SLOTS = (1, 2, 3, 5, 6, 7)
SWAP = (0, 2, 1, 3, 4, 6, 5, 7)
PLANE = (
    (("x", 1), ("x", 3), ("z", 1), ("z", 3)),
    (("x", 3), ("x", 1), ("z", 3), ("z", 1)),
    (("z", 1), ("z", 3), ("x", 1), ("x", 3)),
    (("z", 3), ("z", 1), ("x", 3), ("x", 1)),
)

ORDER = (
    ("dens", 0, 0), ("dens", 1, 0), ("g0", 0, 0), ("g0", 2, 0), ("g1", 0, 0), ("g0", 3, 0),
    ("g0", 1, 0), ("g1", 2, 0), ("g2", 0, 0), ("dens", 2, 0), ("g2", 2, 0), ("dens", 3, 0),
    ("g3", 0, 0), ("g1", 1, 0), ("g1", 3, 0), ("dens", 4, 0), ("dens", 5, 0), ("g3", 2, 0),
    ("col", 0, 0), ("up", 0, 0), ("up", 0, 1), ("col", 2, 0), ("g2", 3, 0), ("s1", 0, 0),
    ("up", 2, 0), ("s1", 0, 1), ("g3", 3, 0), ("up", 2, 1), ("s1", 2, 0), ("s1", 2, 1),
    ("s2", 0, 0), ("col", 3, 0), ("g2", 1, 0), ("up", 3, 0), ("s2", 0, 1), ("g3", 1, 0),
    ("s1", 3, 0), ("s2", 2, 0), ("up", 3, 1), ("s2", 2, 1), ("act", 0, 0), ("s1", 3, 1),
    ("col", 1, 0), ("f1", 0, 0), ("up", 1, 0), ("up", 1, 1), ("f1", 0, 1), ("s1", 1, 0),
    ("act", 2, 0), ("s2", 3, 1), ("s1", 1, 1), ("f1", 2, 0), ("f2", 0, 0), ("s2", 3, 0),
    ("d", 0, 0), ("s2", 1, 0), ("s2", 1, 1), ("act", 3, 0), ("p3", 0, 0), ("f2", 0, 1),
    ("f2", 2, 0), ("f1", 2, 1), ("p2", 0, 0), ("act", 1, 0), ("f1", 3, 0), ("d", 2, 0),
    ("d", 0, 1), ("f1", 3, 1), ("f2", 2, 1), ("p3", 2, 0), ("f1", 1, 0), ("d", 2, 1),
    ("p2", 2, 0), ("p3", 0, 1), ("f2", 3, 0), ("f1", 1, 1), ("f2", 3, 1), ("p3", 2, 1),
    ("d", 3, 0), ("f2", 1, 0), ("d", 3, 1), ("p2", 0, 1), ("p1", 0, 0), ("p2", 2, 1),
    ("f2", 1, 1), ("d", 1, 0), ("p1", 2, 0), ("d", 1, 1), ("p3", 1, 0), ("p3", 3, 0),
    ("p3", 3, 1), ("p3", 1, 1), ("p2", 1, 0), ("p2", 3, 1), ("p2", 3, 0), ("p2", 1, 1),
    ("p0", 2, 0), ("p1", 0, 1), ("p1", 2, 1), ("p1", 3, 1), ("p0", 0, 0), ("p1", 1, 0),
    ("p1", 3, 0), ("p1", 1, 1), ("p0", 1, 0), ("p0", 0, 1), ("p0", 2, 1), ("p0", 3, 1),
    ("p0", 3, 0), ("p0", 1, 1),
)


def flip(value, mask):
    if mask == 0:
        return value
    if mask == 1:
        return value + 1 - 2 * (value % 2)
    if mask == 2:
        return (value + 2) % 4
    return 3 - value


def place():
    wide, narrow = lax.axis_index("wide"), lax.axis_index("narrow")
    return wide // 4, wide % 4, narrow // 2, narrow % 2


def plane_partner(quarter, step, z, x):
    axis, mask = PLANE[quarter][3 - step]
    return (flip(z, mask), x) if axis == "z" else (z, flip(x, mask))


def plane_owner(quarter, position, z, x):
    masks = {"x": 0, "z": 0}
    for step in range(4):
        if position >> step & 1:
            axis, mask = PLANE[quarter][3 - step]
            masks[axis] ^= mask
    return flip(z, masks["z"]), flip(x, masks["x"])


def plane_position(quarter, z_bits, x_bits):
    total = 0
    for step in range(4):
        axis, mask = PLANE[quarter][3 - step]
        high, low = z_bits if axis == "z" else x_bits
        total = total + (high if mask == 3 else (high + low) % 2) * (1 << step)
    return total


def device(z, x, y, core):
    return (z * 4 + x, y * 2 + core)


def greet(partners):
    barrier = pltpu.get_barrier_semaphore()
    for partner in partners:
        pl.semaphore_signal(barrier, inc=1, device_id=partner, device_id_type=MESH)
    pl.semaphore_wait(barrier, len(partners))


def remote(src, dst, send, recv, target):
    return pltpu.make_async_remote_copy(
        src_ref=src, dst_ref=dst, send_sem=send, recv_sem=recv, device_id=target, device_id_type=MESH
    )


def layer_kernel(
    width,
    hidden,
    cap,
    block_rows,
    block_count,
    tok,
    up_rows,
    first_in,
    second_in,
    out,
    grad,
    acts,
    xt,
    xu,
    first,
    second,
    raw_even,
    raw_odd,
    part,
    turned,
    got4,
    got2,
    got1,
    sum3,
    sum2,
    sum1,
    sum0,
    load_sem,
    own_sem,
    sib_send,
    sib_recv,
    a_send,
    a_recv,
    g_send,
    g_recv,
    xt_sem,
    y_send,
    y_recv,
    p_send,
    p_recv,
    acts_sem,
    free_sem,
):
    z, x, y, core = place()
    tile = 256
    up_tile, down_tile = 512, width // 2
    chunk = 16 * ROWS
    piece = width // 4
    source, half = z // 2, z % 2
    sibling = device(z, x, y, 1 - core)
    y_partner = [[device(z, x, flip(y, m), core) for m in (3, 1)], [device(z, x, flip(y, m), core) for m in (1, 3)]]

    raw = (raw_even, raw_odd)

    def load(group):
        return [
            pltpu.make_async_copy(
                ref.at[pl.ds(group * GROUP, GROUP)],
                raw[group % 2].at[a, :, pl.ds(0, cap)],
                load_sem.at[a, group % 2],
            )
            for a, ref in enumerate((first_in, second_in))
        ]

    for group in range(2):
        for copy in load(group):
            copy.start()

    peers = []
    for slot in SLOTS:
        yy = source * flip(y, Y_OF[0][slot % 4]) + (1 - source) * flip(y, Y_OF[1][slot % 4])
        peers.append((yy, 1 - core if slot >= 4 else core))
    greet(
        [device(z, x, yy, cc) for yy, cc in peers]
        + [sibling]
        + [device(flip(z, 1), x, y, core), device(flip(z, 3), x, y, core)]
        + [device(z, flip(x, 1), y, core), device(z, flip(x, 3), y, core)]
    )

    def columns(yy, cc, start, size):
        return pl.ds(pl.multiple_of((yy * 2 + cc) * width + start, 128), size)

    first_copies = [[] for _ in range(PARTS)]
    for t in range(PARTS):
        for s, (yy, cc) in enumerate(peers):
            cols = columns(yy, cc, x * piece, piece)

            def copy(ref, t=t, s=s, yy=yy, cc=cc, cols=cols):
                return remote(
                    ref.at[half, t, :, cols],
                    part.at[0, t, 0, pl.ds(0, ROWS), pl.ds(s * piece, piece)],
                    a_send.at[s, t],
                    a_recv.at[s, t],
                    device(z, x, yy, cc),
                )

            @pl.when(source == 0)
            def _(copy=copy):
                copy(tok).start()

            @pl.when(source == 1)
            def _(copy=copy):
                copy(up_rows).start()

            first_copies[t].append(copy(tok))
    near = []
    for a, ref in enumerate((tok, up_rows)):
        for g in range(2):
            near.append(
                remote(
                    ref.at[g, :, :, columns(y, 1 - core, 0, width)],
                    xu.at[a, :, 4, g],
                    sib_send.at[a, g],
                    sib_recv.at[a, g],
                    sibling,
                )
            )
            near.append(
                pltpu.make_async_copy(
                    ref.at[g, :, :, columns(y, core, 0, width)], xu.at[a, :, 0, g], own_sem.at[a, g]
                )
            )
    for copy in near:
        copy.start()
    for ref in raw:
        ref[:, :, cap] = jnp.zeros((2, GROUP, BLOCK, BLOCK), jnp.bfloat16)

    def place_blocks(group):
        for copy in load(group):
            copy.wait()

        def body(i, _):
            panel = group * GROUP + i
            across = pl.ds(pl.multiple_of(panel * BLOCK, BLOCK), BLOCK)
            for r in range(width // BLOCK):
                slot = cap
                for s in range(cap):
                    hit = jnp.logical_and(block_rows[s, panel] == r, s < block_count[panel])
                    slot = jnp.where(hit, s, slot)
                first[r * BLOCK : (r + 1) * BLOCK, across] = raw[group % 2][0, i, slot]
                second[across, r * BLOCK : (r + 1) * BLOCK] = raw[group % 2][1, i, slot]
            return 0

        lax.fori_loop(0, GROUP, body, 0)
        if group + 2 < hidden // BLOCK // GROUP:
            for copy in load(group + 2):
                copy.start()

    def gather_copies(t, step):
        copies = []
        for u in range(3):
            cols = pl.ds(u * 2 * piece, 2 * piece)
            low, high = pl.ds(0, ROWS), pl.ds(ROWS, ROWS)
            if step == 0:
                src, dst = part.at[0, t, 0, low, cols], part.at[0, t, 0, high, cols]
            else:
                size = 1 << (step - 1)
                src = part.at[0, t, pl.ds(0, size), :, cols]
                dst = part.at[0, t, pl.ds(size, size), :, cols]
            zz, xx = plane_partner((t + u) % 4, step, z, x)
            copies.append(
                remote(src, dst, g_send.at[step, t, u], g_recv.at[step, t, u], device(zz, xx, y, core))
            )
        return copies

    def gather(t, step):
        if step == 0:
            for copy in first_copies[t]:
                copy.wait()
        if step > 0:
            for copy in gather_copies(t, step - 1):
                copy.wait()
        for copy in gather_copies(t, step):
            copy.start()

    def collect(t):
        for copy in gather_copies(t, 3):
            copy.wait()
        while near:
            near.pop().wait()
        for u in range(3):
            for position in range(16):
                zz, xx = plane_owner((t + u) % 4, position, z, x)
                cols = pl.ds(pl.multiple_of(xx * piece, 128), piece)
                for s in (2 * u, 2 * u + 1):
                    xu[zz // 2, t, SLOTS[s], zz % 2, :, cols] = part[
                        0,
                        t,
                        position // 2,
                        (position % 2) * ROWS : (position % 2 + 1) * ROWS,
                        s * piece : (s + 1) * piece,
                    ]

    turning = []

    def turn_copies(t):
        cols = pl.ds(t * chunk, chunk)
        return [pltpu.make_async_copy(turned.at[a], xt.at[a, :, cols], xt_sem.at[a]) for a in range(2)]

    def turn_inputs(t):
        while turning:
            turning.pop().wait()
        for a in range(2):
            turned[a] = xu[a, t].reshape(chunk, width).T
        for copy in turn_copies(t):
            copy.start()
            turning.append(copy)

    def sums_copy(step, a, t):
        if step == 2:
            src, dst, to = part.at[a, t, pl.ds(4, 4)], got4.at[a, t], sibling
        elif step == 1:
            src, dst, to = part.at[a, t, pl.ds(2, 2)], got2.at[a, t], y_partner[a][1]
        else:
            src, dst, to = part.at[a, t, pl.ds(1, 1)], got1.at[a, t], y_partner[a][0]
        return remote(src, dst, y_send.at[step, a, t], y_recv.at[step, a, t], to)

    def back_copy(step, a, t):
        to = sibling if step == 2 else y_partner[a][step]
        size = 1 << step
        return remote(
            part.at[a, t, pl.ds(0, size)],
            part.at[a, t, pl.ds(size, size)],
            y_send.at[3 + step, a, t],
            y_recv.at[3 + step, a, t],
            to,
        )

    def sums_arrive(step, a, t):
        sums_copy(step, a, t).wait()
        to = sibling if step == 2 else y_partner[a][step]
        pl.semaphore_signal(free_sem.at[step, a, t], inc=1, device_id=to, device_id_type=MESH)

    def send_back(step, a, t):
        pl.semaphore_wait(free_sem.at[step, a, t], 1)
        back_copy(step, a, t).start()

    def plane_copy(step, a, q, t):
        rows = pl.ds(q * ROWS, ROWS)
        buffer = got4.at[a, t]
        if step == 3:
            src, dst = buffer.at[pl.ds(2, 2), rows, :], sum3.at[a, t, :, rows, :]
        elif step == 2:
            src, dst = buffer.at[pl.ds(1, 1), rows, :], sum2.at[a, t, :, rows, :]
        elif step == 1:
            src, dst = buffer.at[0, rows, pl.ds(width, width)], sum1.at[a, t, rows, :]
        else:
            src, dst = buffer.at[0, rows, pl.ds(width // 2, width // 2)], sum0.at[a, t, rows, :]
        zz, xx = plane_partner(a * 2 + q, step, z, x)
        return remote(
            src, dst, p_send.at[step, a, q, t], p_recv.at[step, a, q, t], device(zz, xx, y, core)
        )

    def up(t, a):

        def body(j, _, a=a):
            cols = pl.ds(pl.multiple_of(j * up_tile, up_tile), up_tile)
            rows = xu[a, t].reshape(chunk, width)
            if a == 0:
                value = jnp.dot(rows, first[:, cols], preferred_element_type=jnp.float32)
            else:
                value = lax.dot_general(
                    rows, second[cols, :], (((1,), (1,)), ((), ())), preferred_element_type=jnp.float32
                )
            value = value.astype(jnp.bfloat16).reshape(8, 2 * ROWS, up_tile)
            for i in range(8):
                part[a, t, SWAP[i], :, cols] = value[i]
            return 0

        lax.fori_loop(0, hidden // up_tile, body, 0)
        sums_copy(2, a, t).start()

    def add_into(t, a, step):
        got = (got1, got2, got4)[step]
        size = 1 << step
        sums_arrive(step, a, t)

        def body(j, _, a=a):
            cols = pl.ds(pl.multiple_of(j * tile, tile), tile)
            total = part[a, t, :size, :, cols].astype(jnp.float32) + got[a, t, :, :, cols].astype(jnp.float32)
            part[a, t, :size, :, cols] = total.astype(jnp.bfloat16)
            return 0

        lax.fori_loop(0, hidden // tile, body, 0)
        sums_copy(step - 1, a, t).start()

    def activate(t):
        for a in range(2):
            sums_arrive(0, a, t)

        def body(j, _):
            cols = pl.ds(pl.multiple_of(j * tile, tile), tile)

            def whole(a):
                return part[a, t, 0, :, cols].astype(jnp.float32) + got1[a, t, 0, :, cols].astype(jnp.float32)

            v, g = whole(0), whole(1)
            scale = math.sqrt(2 / math.pi)
            square = v * v
            th = jnp.tanh(scale * (v + 0.044715 * square * v))
            slope = 0.5 * (1 + th) + 0.5 * v * (1 - th * th) * (scale * (1 + 3 * 0.044715 * square))
            part[0, t, 0, :, cols] = (0.5 * v * (1 + th)).astype(jnp.bfloat16)
            part[1, t, 0, :, cols] = (g * slope).astype(jnp.bfloat16)
            return 0

        lax.fori_loop(0, hidden // tile, body, 0)
        for a in range(2):
            send_back(0, a, t)
        turn_inputs(t)

    def forward(t, a, step):
        back_copy(step - 1, a, t).wait()
        send_back(step, a, t)

    def down(t, a):
        back_copy(2, a, t).wait()
        pltpu.make_async_copy(part.at[a, t], acts.at[a, t], acts_sem.at[a, t]).start()
        for q in range(2):
            spots = []
            for i in range(8):
                yy = flip(y, Y_OF[a][i % 4])
                cc = 1 - core if i >= 4 else core
                z_bits = ((yy // 2 + z // 2) % 2, (yy + z) % 2)
                for r in range(2):
                    x_bits = ((cc + x // 2) % 2, (r + x) % 2)
                    spots.append(plane_position(a * 2 + q, z_bits, x_bits))

            def body(a=a, q=q, spots=spots):
                cols = pl.ds(pl.multiple_of(q * down_tile, down_tile), down_tile)
                rows = part[a, t].reshape(chunk, hidden)
                if a == 0:
                    value = jnp.dot(rows, second[:, cols], preferred_element_type=jnp.float32)
                else:
                    value = lax.dot_general(
                        rows, first[cols, :], (((1,), (1,)), ((), ())), preferred_element_type=jnp.float32
                    )
                value = value.astype(jnp.bfloat16).reshape(16, ROWS, down_tile)
                for i, spot in enumerate(spots):
                    at = pl.ds(pl.multiple_of((spot % 4) * down_tile, down_tile), down_tile)
                    got4[a, t, spot // 4, pl.ds(q * ROWS, ROWS), at] = value[i]

            body()
            plane_copy(3, a, q, t).start()

    def plane_add(t, a, step):
        for q in range(2):
            plane_copy(step, a, q, t).wait()
        cols = pl.ds(0, {3: hidden, 2: hidden, 1: width, 0: width // 2}[step])
        if step == 3:
            for i in range(2):
                got4[a, t, i] = (
                    got4[a, t, i].astype(jnp.float32) + sum3[a, t, i].astype(jnp.float32)
                ).astype(jnp.bfloat16)
        else:
            mine = got4[a, t, 0, :, cols].astype(jnp.float32)
            theirs = sum2[a, t, 0] if step == 2 else (sum1 if step == 1 else sum0)[a, t]
            total = (mine + theirs.astype(jnp.float32)).astype(jnp.bfloat16)
            if step:
                got4[a, t, 0, :, cols] = total
            else:
                for q in range(2):
                    (out, grad)[a][pl.ds(t * ROWS, ROWS), pl.ds(q * (width // 2), width // 2)] = total[
                        q * ROWS : (q + 1) * ROWS
                    ]
        if step:
            for q in range(2):
                plane_copy(step - 1, a, q, t).start()

    stages = {
        "up": up,
        "s1": lambda t, a: add_into(t, a, 2),
        "s2": lambda t, a: add_into(t, a, 1),
        "act": lambda t, a: activate(t),
        "f1": lambda t, a: forward(t, a, 1),
        "f2": lambda t, a: forward(t, a, 2),
        "d": down,
        "dens": lambda group, a: place_blocks(group),
        "col": lambda t, a: collect(t),
    }
    for step in range(4):
        stages[f"g{step}"] = lambda t, a, step=step: gather(t, step)
        stages[f"p{step}"] = lambda t, a, step=step: plane_add(t, a, step)
    for name, t, a in ORDER:
        stages[name](t, a)
    for t in range(PARTS):
        for a in range(2):
            pltpu.make_async_copy(part.at[a, t], acts.at[a, t], acts_sem.at[a, t]).wait()
    while turning:
        turning.pop().wait()


def layer(tokens, upstream, first_blocks, second_blocks, rows_of, count):
    local, total = tokens.shape
    panels, cap = first_blocks.shape[:2]
    width, hidden = total // 8, panels * BLOCK
    split = (2, PARTS, local // 2 // PARTS, total)
    dma = pltpu.SemaphoreType.DMA

    def vmem(*shape):
        return pltpu.VMEM(shape, jnp.bfloat16)

    pair, rows = (2, PARTS), 2 * ROWS
    inputs = (*pair, 8, 2, ROWS, width)
    whole = jax.ShapeDtypeStruct((64, width), jnp.bfloat16)
    anywhere = pl.BlockSpec(memory_space=pl.ANY)
    scalars = pl.BlockSpec(memory_space=pltpu.SMEM)
    on_chip = pl.BlockSpec(memory_space=pltpu.VMEM)
    return pl.pallas_call(
        functools.partial(layer_kernel, width, hidden, cap),
        out_shape=[
            whole,
            whole,
            jax.ShapeDtypeStruct((*pair, 8, rows, hidden), jnp.bfloat16),
            jax.ShapeDtypeStruct((2, width, 16 * ROWS * PARTS), jnp.bfloat16),
        ],
        in_specs=[scalars, scalars] + [anywhere] * 4,
        out_specs=[on_chip, on_chip, anywhere, anywhere],
        scratch_shapes=[
            vmem(*inputs),
            vmem(width, hidden),
            vmem(hidden, width),
            vmem(2, GROUP, cap + 1, BLOCK, BLOCK),
            vmem(2, GROUP, cap + 1, BLOCK, BLOCK),
            vmem(*pair, 8, rows, hidden),
            vmem(2, width, 16 * ROWS),
            vmem(*pair, 4, rows, hidden),
            vmem(*pair, 2, rows, hidden),
            vmem(*pair, 1, rows, hidden),
            vmem(*pair, 2, rows, hidden),
            vmem(*pair, 1, rows, hidden),
            vmem(*pair, rows, width),
            vmem(*pair, rows, width // 2),
            dma((2, 2)),
            dma((2, 2)),
            dma((2, 2)),
            dma((2, 2)),
            dma((6, PARTS)),
            dma((6, PARTS)),
            dma((4, PARTS, 3)),
            dma((4, PARTS, 3)),
            dma((2,)),
            dma((6, *pair)),
            dma((6, *pair)),
            dma((4, 2, 2, PARTS)),
            dma((4, 2, 2, PARTS)),
            dma(pair),
            pltpu.SemaphoreType.REGULAR((3, *pair)),
        ],
        compiler_params=pltpu.CompilerParams(
            collective_id=1, has_side_effects=True, vmem_limit_bytes=VMEM_LIMIT
        ),
    )(rows_of, count, tokens.reshape(split), upstream.reshape(split), first_blocks, second_blocks)


def grads_kernel(rows, count, xt, acts, first_grad, second_grad):
    panel = pl.program_id(0)
    cap = first_grad.shape[1]

    def one(p, _):
        at_panel = pl.ds(pl.multiple_of(p * BLOCK, BLOCK), BLOCK)
        index = panel * first_grad.shape[0] + p
        for kept in range(1, cap + 1):

            @pl.when(count[index] == kept)
            def _(kept=kept):
                for a, grad in ((0, first_grad), (1, second_grad)):
                    blocks = [
                        xt[a, pl.ds(pl.multiple_of(rows[slot, index] * BLOCK, BLOCK), BLOCK), :]
                        for slot in range(kept)
                    ]
                    value = jnp.dot(
                        jnp.concatenate(blocks), acts[1 - a, :, at_panel], preferred_element_type=jnp.float32
                    )
                    for slot in range(cap):
                        if slot >= kept:
                            grad[p, slot] = jnp.zeros((BLOCK, BLOCK), jnp.float32)
                        else:
                            block = value[slot * BLOCK : (slot + 1) * BLOCK]
                            grad[p, slot] = block.T if a else block

        return 0

    lax.fori_loop(0, first_grad.shape[0], one, 0)


def weight_grads(xt, acts, rows, count):
    cap, panels = rows.shape
    _, width, tokens = xt.shape
    block = pl.BlockSpec((GROUP, cap, BLOCK, BLOCK), lambda j, *_: (j, 0, 0, 0))
    result = jax.ShapeDtypeStruct((panels, cap, BLOCK, BLOCK), jnp.float32)
    return pl.pallas_call(
        grads_kernel,
        grid_spec=pltpu.PrefetchScalarGridSpec(
            num_scalar_prefetch=2,
            grid=(panels // GROUP,),
            in_specs=[
                pl.BlockSpec((2, width, tokens), lambda j, *_: (0, 0, 0)),
                pl.BlockSpec((2, tokens, GROUP * BLOCK), lambda j, *_: (0, 0, j)),
            ],
            out_specs=[block, block],
        ),
        out_shape=[result, result],
        compiler_params=pltpu.CompilerParams(vmem_limit_bytes=VMEM_LIMIT),
    )(rows, count, xt, acts.reshape(2, tokens, panels * BLOCK))


def on_device(tokens, first_blocks, second_blocks, block_rows, block_count, upstream):
    rows, count = block_rows.T, block_count.reshape(-1)
    layer_output, grad_tokens, acts, xt = layer(tokens, upstream, first_blocks, second_blocks, rows, count)
    first_grad, second_grad = weight_grads(xt, acts, rows, count)
    return layer_output, grad_tokens, first_grad, second_grad


def solution(mesh):
    blocks = P("wide", "narrow", None, None)
    return jax.shard_map(
        on_device,
        mesh=mesh,
        in_specs=(P("narrow", None), blocks, blocks, P("wide", "narrow"), P("wide", "narrow"), P("narrow", None)),
        out_specs=(P("wide", "narrow"), P("wide", "narrow"), blocks, blocks),
        check_vma=False,
    )
```
